128 devices in a mesh: req: 8 (over y_lo, x), patch: 16 (over y_hi, z, core).
Axes of the slice: x: 4, y: 4 (y_hi: 2, y_lo: 2; y = y_hi * 2 + y_lo), z: 4, core: 2. Of those that a mesh axis runs over, the one named last changes fastest.
Arguments:
- latent: bfloat16 [16384, 1536], P(('req', 'patch')), parts along dimension 0, may hold values from -6 to 6
- stale_kv: bfloat16 [16384, 3072], P(('req', 'patch')), parts along dimension 0, may hold values from -6 to 6
- timesteps: int32 [16], P('req'), parts along dimension 0, may hold values from 0 to 999
- counts: int32 [128], P('req'), parts along dimension 0, may hold values from 1 to 128, as said below
- conv_weight: float32 [3, 1536], replicated, may hold values from -3 to 3
- w_mod: float32 [256, 4608], replicated, may hold values from -0.375 to 0.375
- w_qkv: bfloat16 [1536, 4608], replicated
- q_gain: float32 [1536], replicated, may hold values from 0.5 to 4.5
- k_gain: float32 [1536], replicated, may hold values from 0.5 to 4.5
- w_out: bfloat16 [1536, 1536], replicated, may hold values from -0.15625 to 0.15625
Outputs:
- latent_out: bfloat16 [16384, 1536], P(('req', 'patch')), parts along dimension 0
- next_cache: bfloat16 [16384, 3072], P(('req', 'patch')), parts along dimension 0
The draws below stay inside these ranges and needn't reach their ends.
There are 8 independent parts, one for each index of `req`. The reference program is written for one: setup_inputs(seed, part) draws one part's arguments, and reference() takes and returns one part's arrays. A program takes and returns all parts, laid end to end along the dimension named above; an argument that names none is the same for every part. Nothing has to cross between parts.
Inputs may be any that keep to these rules, and one draw needn't show every extreme that they name: `counts`: some slab holds 128 live tokens.
All inputs are finite; a program needn't handle non-finite values.
Results may differ from the reference program's by a relative error of at most 0.0085.
Values may be sent and summed in bfloat16 or wider, within the bound.
No kernel may reach another device: no remote copies, remote signals or barrier semaphores. Data moves between devices by JAX's collectives and lax.ppermute only.
A program may use at most 192 MiB of HBM per device.

```python
import math
import jax
import jax.numpy as jnp
from jax import lax

D = 1536
HEADS = 12
HEAD = 128
FREQ = 256
FRAME = 80
STEPS = 2
TOK_DEV = 128
TOKENS = 2048
SLABS = 16


def draw_w_qkv(key, part):
    key = jax.random.fold_in(key, 11)
    first_key = jax.random.fold_in(key, 0)
    head_total = HEADS * HEAD
    base_draw = jax.random.normal(first_key, (D, 3 * head_total), jnp.float32) * D ** (-0.5)
    return base_draw.astype(jnp.bfloat16)


def draw_q_gain(key, part):
    key = jax.random.fold_in(key, 12)
    return jnp.exp(jax.random.uniform(key, (HEADS * HEAD,), jnp.float32, math.log(0.5), math.log(2.0)))


def draw_k_gain(key, part):
    key = jax.random.fold_in(key, 13)
    return jnp.exp(jax.random.uniform(key, (HEADS * HEAD,), jnp.float32, math.log(0.5), math.log(2.0)))


def draw_counts(key, part):
    key = jax.random.fold_in(key, 14)
    count_key, place_key = jax.random.split(key)
    ragged = jax.random.randint(count_key, (SLABS,), 1, TOK_DEV + 1, jnp.int32)
    full_place = jax.random.randint(place_key, (), 0, SLABS, jnp.int32)
    places = jnp.arange(SLABS, dtype=jnp.int32)
    return jnp.where(places == full_place, TOK_DEV, ragged).astype(jnp.int32)


def shard_levels(key, extent, shards, least, high):
    loudness = 1.0
    for position, parts in shards:
        steps = jax.random.uniform(jax.random.fold_in(jax.random.fold_in(key, 6), position), (parts,), jnp.float32, least / len(shards), high / len(shards))
        loudness = loudness * jnp.repeat(jnp.exp(steps), extent[position] // parts).reshape((-1,) + (1,) * (len(extent) - 1 - position))
    return loudness


def gaussian(own_key, dims, spread, most, shards=(), held_as=jnp.bfloat16):
    result = spread * jax.random.normal(own_key, dims, jnp.float32)
    if shards:
        result = result * shard_levels(own_key, dims, shards, -0.22, 0.18)
    return jnp.clip(result, -most, most).astype(held_as)


def setup_inputs(seed: int = 0, part: int = 0) -> dict:
    keys = jax.random.split(jax.random.key(seed), 11)
    part_keys = jax.random.split(jax.random.fold_in(keys[10], part), 11)
    latent = gaussian(part_keys[0], (TOKENS, D), 1.0, 6.0, ((0, 16),))
    stale_kv = gaussian(part_keys[1], (TOKENS, 2 * HEADS * HEAD), 1.0, 6.0, ((0, 16),))
    timesteps = jax.random.randint(part_keys[2], (STEPS,), 0, 1000).astype(jnp.int32)
    counts = draw_counts(jax.random.fold_in(jax.random.fold_in(keys[10], part), 71), part)
    conv_weight = gaussian(keys[4], (3, D), 0.5, 3.0, (), jnp.float32)
    w_mod = gaussian(keys[5], (FREQ, 3 * D), FREQ ** -0.5, 0.375, (), jnp.float32)
    w_qkv = draw_w_qkv(jax.random.fold_in(keys[10], 71), part)
    q_gain = draw_q_gain(jax.random.fold_in(keys[10], 71), part)
    k_gain = draw_k_gain(jax.random.fold_in(keys[10], 71), part)
    w_out = gaussian(keys[9], (HEADS * HEAD, D), (HEADS * HEAD) ** -0.5, 0.15625)
    return dict(latent=latent, stale_kv=stale_kv, timesteps=timesteps, counts=counts, conv_weight=conv_weight, w_mod=w_mod, w_qkv=w_qkv, q_gain=q_gain, k_gain=k_gain, w_out=w_out)


epsilon = 1e-06
masked_score = -1e+30

def embedding(moment):
    halfway = FREQ // 2
    frequency = jnp.exp(-math.log(10000.0) * jnp.arange(halfway, dtype=jnp.float32) / halfway)
    angles = moment.astype(jnp.float32) * frequency
    return jnp.concatenate([jnp.cos(angles), jnp.sin(angles)])

def modulation(moment, w_mod):
    activated = jax.nn.silu(embedding(moment))[None, :]
    mod_terms = jnp.dot(activated, w_mod, precision=lax.Precision.HIGHEST, preferred_element_type=jnp.float32)[0]
    features = w_mod.shape[1] // 3
    return (mod_terms[:features], mod_terms[features:2 * features], mod_terms[2 * features:])

def layer_normed(mixed_rows, shift_vec, scale_vec):
    centred = mixed_rows - lax.optimization_barrier(jnp.mean(mixed_rows, -1, keepdims=True))
    variance = lax.optimization_barrier(jnp.mean(centred * centred, -1, keepdims=True))
    return (centred * lax.rsqrt(variance + epsilon) * (1.0 + scale_vec) + shift_vec).astype(jnp.bfloat16)

def head_normed(projected, gain, heads_count):
    count_rows = projected.shape[0]
    split_rows = projected.reshape(count_rows, heads_count, -1)
    mean_square = lax.optimization_barrier(jnp.mean(split_rows * split_rows, -1, keepdims=True))
    return (split_rows * lax.rsqrt(mean_square + epsilon) * gain.reshape(heads_count, -1)).astype(jnp.bfloat16)

def convolved(hidden_state, conv_weight, padded):
    count_rows = hidden_state.shape[0]
    as_float = hidden_state.astype(jnp.float32)
    before = padded[:count_rows].astype(jnp.float32)
    after_rows = padded[2 * FRAME:].astype(jnp.float32)
    return as_float + conv_weight[0] * before + conv_weight[1] * as_float + conv_weight[2] * after_rows

def denoise_block(hidden_state, old_keys, old_values, moment, counts, conv_weight, w_mod, w_qkv, q_gain, k_gain, w_out):
    padded = jnp.pad(hidden_state, ((FRAME, FRAME), (0, 0)))
    mixed_rows = convolved(hidden_state, conv_weight, padded)
    shift_vec, scale_vec, gate_vec = modulation(moment, w_mod)
    normed = layer_normed(mixed_rows, shift_vec, scale_vec)
    head_total = HEADS * HEAD
    projected = jnp.dot(normed, w_qkv, preferred_element_type=jnp.float32)
    queries = head_normed(projected[:, :head_total], q_gain, HEADS)
    fresh_keys = head_normed(projected[:, head_total:2 * head_total], k_gain, HEADS)
    fresh_values = projected[:, 2 * head_total:].reshape(TOKENS, HEADS, HEAD).astype(jnp.bfloat16)
    positions = jnp.arange(TOKENS, dtype=jnp.int32)
    key_slab = positions // TOK_DEV
    live_keys = positions - key_slab * TOK_DEV < counts[key_slab]
    scaling = 1.0 / math.sqrt(HEAD)

    def one_slab(slab_index):
        own_keys = key_slab == slab_index
        keys_used = jnp.where(own_keys[:, None, None], fresh_keys, old_keys)
        values_used = jnp.where(own_keys[:, None, None], fresh_values, old_values)
        slab_queries = lax.dynamic_slice_in_dim(queries, (slab_index * TOK_DEV).astype(jnp.int32), TOK_DEV, 0)
        scores = jnp.einsum('qhd,khd->qhk', slab_queries.astype(jnp.float32), keys_used.astype(jnp.float32)) * scaling
        scores = jnp.where(live_keys[None, None, :], scores, masked_score)
        weights = jax.nn.softmax(scores, -1).astype(jnp.bfloat16)
        return jnp.einsum('qhk,khd->qhd', weights.astype(jnp.float32), values_used.astype(jnp.float32)).astype(jnp.bfloat16)
    attended = lax.map(one_slab, jnp.arange(SLABS, dtype=jnp.int32)).reshape(TOKENS, head_total)
    output_rows = jnp.dot(attended, w_out, preferred_element_type=jnp.float32)
    next_state = (mixed_rows + gate_vec * output_rows).astype(jnp.bfloat16)
    return (next_state, fresh_keys, fresh_values)

def reference(latent, stale_kv, timesteps, counts, conv_weight, w_mod, w_qkv, q_gain, k_gain, w_out):
    head_total = HEADS * HEAD
    old_keys = stale_kv[:, :head_total].reshape(TOKENS, HEADS, HEAD)
    old_values = stale_kv[:, head_total:].reshape(TOKENS, HEADS, HEAD)
    hidden_state = latent
    for step_index in range(STEPS):
        hidden_state, old_keys, old_values = denoise_block(hidden_state, old_keys, old_values, timesteps[step_index], counts, conv_weight, w_mod, w_qkv, q_gain, k_gain, w_out)
    next_cache = jnp.concatenate([old_keys.reshape(TOKENS, head_total), old_values.reshape(TOKENS, head_total)], 1)
    return (hidden_state, next_cache)
```

```python
import math

import jax
import jax.numpy as jnp
from jax import lax
from jax.experimental import pallas as pl
from jax.experimental.pallas import tpu as pltpu
from jax.sharding import PartitionSpec as P

HEAD = 128
FREQ = 256
FRAME = 80
STEPS = 2
SLAB = 128
D = 1536
GROUP = 3
WIDE = GROUP * HEAD
RING = 4
LOG2E = math.log2(math.e)

epsilon = 1e-06
masked_score = -1e30
f32 = jnp.float32
bf16 = jnp.bfloat16


def place(y, z, c):
    return 8 * y + 2 * z + c


DEVICES = [(y, z, c) for y in range(2) for z in range(RING) for c in range(2)]
CORE = [(place(y, z, c), place(y, z, 1 - c)) for y, z, c in DEVICES]
ACROSS = [(place(y, z, c), place(1 - y, z, c)) for y, z, c in DEVICES]


def ring(k):
    return [(place(y, z, c), place(y, (z + k) % RING, c)) for y, z, c in DEVICES]


NEXT_CHIP = [(p, p + 1) for p in range(1, 15, 2)] + [(p + 1, p) for p in range(1, 15, 2)]


def params(megabytes=48):
    return pltpu.CompilerParams(vmem_limit_bytes=megabytes * 2**20)


def embedding(moment):
    halfway = FREQ // 2
    frequency = jnp.exp(-math.log(10000.0) * jnp.arange(halfway, dtype=f32) / halfway)
    angles = moment.astype(f32) * frequency
    return jnp.concatenate([jnp.cos(angles), jnp.sin(angles)])


def modulation_kernel(active_ref, w_ref, out_ref):
    out_ref[...] = jnp.dot(
        active_ref[...], w_ref[...], precision=lax.Precision.HIGHEST, preferred_element_type=f32
    )


def modulation(timesteps, w_mod):
    rows = jnp.stack([jax.nn.silu(embedding(timesteps[s])) for s in range(STEPS)])
    active = jnp.concatenate([rows, jnp.zeros((8 - STEPS, FREQ), f32)], 0)
    columns = w_mod.shape[1]
    tile = columns // 6
    return pl.pallas_call(
        modulation_kernel,
        grid=(6,),
        in_specs=[
            pl.BlockSpec((8, FREQ), lambda i: (0, 0)),
            pl.BlockSpec((FREQ, tile), lambda i: (0, i)),
        ],
        out_specs=pl.BlockSpec((8, tile), lambda i: (0, i)),
        out_shape=jax.ShapeDtypeStruct((8, columns), f32),
        compiler_params=params(),
        name="modulation",
    )(active, w_mod)


def split_kernel(place_ref, keys_ref, values_ref, *out_refs):
    step = pl.program_id(0)
    for k in range(RING):

        @pl.when(step == k)
        def _():
            out_refs[k][:, :WIDE] = keys_ref[...]
            out_refs[k][:, WIDE:] = values_ref[...]


def split_cache(where, stale_kv):
    return pl.pallas_call(
        split_kernel,
        grid_spec=pltpu.PrefetchScalarGridSpec(
            num_scalar_prefetch=1,
            grid=(RING,),
            in_specs=[
                pl.BlockSpec((SLAB, WIDE), lambda i, p: (0, (p[0] + i) % RING)),
                pl.BlockSpec((SLAB, WIDE), lambda i, p: (0, RING + (p[0] + i) % RING)),
            ],
            out_specs=[pl.BlockSpec((SLAB, 2 * WIDE), lambda i, p: (0, 0))] * RING,
        ),
        out_shape=[jax.ShapeDtypeStruct((SLAB, 2 * WIDE), bf16)] * RING,
        compiler_params=params(),
        name="split_cache",
    )(where, stale_kv, stale_kv)


def head_normed(block, gain):
    mean_square = jnp.mean(block * block, -1, keepdims=True)
    return (block * lax.rsqrt(mean_square + epsilon) * gain).astype(bf16)


def project_kernel(
    place_ref, state_ref, core_ref, chip_ref, conv_ref, mod_ref, q_gain_ref, k_gain_ref,
    wq_ref, wk_ref, wv_ref, out0, out1, out2, out3, cache_ref, mixed_ref, normed_ref, *, row
):
    outs = (out0, out1, out2, out3)
    step = pl.program_id(0)
    core = place_ref[1]

    @pl.when(step == 0)
    def _():
        state = state_ref[...].astype(f32)
        core_rows = core_ref[...].astype(f32)
        chip_rows = chip_ref[...].astype(f32)
        first = core == 0
        above = jnp.where(first, chip_rows, core_rows)
        below = jnp.where(first, core_rows, chip_rows)
        before = jnp.concatenate([above, state[: SLAB - FRAME]], 0)
        after_rows = jnp.concatenate([state[FRAME:], below], 0)
        mixed = (
            state
            + conv_ref[0:1, :] * before
            + conv_ref[1:2, :] * state
            + conv_ref[2:3, :] * after_rows
        )
        mixed_ref[...] = mixed
        shift = mod_ref[row : row + 1, :D]
        scale = mod_ref[row : row + 1, D : 2 * D]
        centred = mixed - jnp.mean(mixed, -1, keepdims=True)
        variance = jnp.mean(centred * centred, -1, keepdims=True)
        normed_ref[...] = (
            centred * lax.rsqrt(variance + epsilon) * (1.0 + scale) + shift
        ).astype(bf16)

    normed = normed_ref[...]
    queries = jnp.dot(normed, wq_ref[...], preferred_element_type=f32)
    keys = jnp.dot(normed, wk_ref[...], preferred_element_type=f32)
    values = jnp.dot(normed, wv_ref[...], preferred_element_type=f32).astype(bf16)
    pieces = []
    for block, gain_ref in ((queries, q_gain_ref), (keys, k_gain_ref)):
        for h in range(GROUP):
            columns = slice(h * HEAD, (h + 1) * HEAD)
            pieces.append(head_normed(block[:, columns], gain_ref[:, columns]))
    queries, keys = jnp.concatenate(pieces[:GROUP], 1), jnp.concatenate(pieces[GROUP:], 1)
    group = (place_ref[0] + step) % RING
    start = pl.multiple_of(group * WIDE, WIDE)
    cache_ref[:, pl.ds(start, WIDE)] = keys
    cache_ref[:, pl.ds(pl.multiple_of(start + D, WIDE), WIDE)] = values
    for k in range(RING):

        @pl.when(step == k)
        def _():
            outs[k][:, :WIDE] = queries
            outs[k][:, WIDE : 2 * WIDE] = keys
            outs[k][:, 2 * WIDE :] = values


def project(where, state, core_rows, chip_rows, conv_weight, mod, q_gain, k_gain, w_qkv, row):
    def whole(shape):
        return pl.BlockSpec(shape, lambda i, p: (0, 0))

    def weight(part):
        return pl.BlockSpec((D, WIDE), lambda i, p: (0, part * RING + (p[0] + i) % RING))

    gain = pl.BlockSpec((1, WIDE), lambda i, p: (0, (p[0] + i) % RING))

    def body(*refs):
        project_kernel(*refs, row=row)

    return pl.pallas_call(
        body,
        grid_spec=pltpu.PrefetchScalarGridSpec(
            num_scalar_prefetch=1,
            grid=(RING,),
            in_specs=[
                whole((SLAB, D)),
                whole((FRAME, D)),
                whole((FRAME, D)),
                whole((3, D)),
                whole((8, 3 * D)),
                gain,
                gain,
                weight(0),
                weight(1),
                weight(2),
            ],
            out_specs=[whole((SLAB, 3 * WIDE))] * RING + [whole((SLAB, 2 * D)), whole((SLAB, D))],
            scratch_shapes=[pltpu.VMEM((SLAB, D), bf16)],
        ),
        out_shape=[jax.ShapeDtypeStruct((SLAB, 3 * WIDE), bf16)] * RING
        + [jax.ShapeDtypeStruct((SLAB, 2 * D), bf16), jax.ShapeDtypeStruct((SLAB, D), f32)],
        compiler_params=params(),
        name="project",
    )(
        where, state, core_rows, chip_rows, conv_weight, mod,
        q_gain.reshape(1, -1), k_gain.reshape(1, -1), w_qkv, w_qkv, w_qkv,
    )


def scores_of(queries, keys, bias):
    dots = lax.dot_general(
        queries, keys, (((1,), (1,)), ((), ())), preferred_element_type=f32
    )
    return dots * (LOG2E / math.sqrt(HEAD)) + bias


def attend_kernel(*refs):
    q_refs, k_refs, v_refs = refs[0:4], refs[4:8], refs[8:12]
    old_k, old_v = refs[12:16], refs[16:20]
    bias_ref = refs[20]
    outs = refs[21:25]
    scores, weights, own = refs[25:28]
    rows = RING * SLAB
    queries = jnp.concatenate([q[...] for q in q_refs], 0)
    for a in range(4):
        scores[:, a * rows : (a + 1) * rows] = scores_of(
            queries, old_k[a][...], bias_ref[a : a + 1, :]
        )
    for j in range(RING):
        here = slice(j * SLAB, (j + 1) * SLAB)
        scores[here, here] = scores_of(q_refs[j][...], k_refs[j][...], bias_ref[0:1, here])
    for j in range(RING):
        here = slice(j * SLAB, (j + 1) * SLAB)
        block = scores[here, :]
        highest = jnp.max(block, -1, keepdims=True)
        probs = jnp.exp2(block - highest)
        total = jnp.sum(probs, -1, keepdims=True)
        weights[here, :] = probs.astype(bf16)
        own[here, :] = weights[here, here]
        weights[here, here] = jnp.zeros((SLAB, SLAB), bf16)
        summed = jnp.dot(own[here, :], v_refs[j][...], preferred_element_type=f32)
        for a in range(4):
            summed += jnp.dot(
                weights[here, a * rows : (a + 1) * rows], old_v[a][...], preferred_element_type=f32
            )
        outs[j][...] = (summed / total).astype(bf16)


def attend(fresh, olds, bias):
    rows = RING * SLAB

    def column(n, part):
        return pl.BlockSpec((n, HEAD), lambda h: (0, part * GROUP + h))

    return pl.pallas_call(
        attend_kernel,
        grid=(GROUP,),
        in_specs=[column(SLAB, 0)] * 4
        + [column(SLAB, 1)] * 4
        + [column(SLAB, 2)] * 4
        + [column(rows, 0)] * 4
        + [column(rows, 1)] * 4
        + [pl.BlockSpec((4, rows), lambda h: (0, 0))],
        out_specs=[column(SLAB, 0)] * 4,
        out_shape=[jax.ShapeDtypeStruct((SLAB, WIDE), bf16)] * 4,
        scratch_shapes=[
            pltpu.VMEM((rows, 4 * rows), f32),
            pltpu.VMEM((rows, 4 * rows), bf16),
            pltpu.VMEM((rows, SLAB), bf16),
        ],
        compiler_params=params(),
        name="attend",
    )(*fresh, *fresh, *fresh, *olds, *olds, bias)


def output_kernel(place_ref, a0, a1, a2, a3, w0, w1, w2, w3, mixed_ref, gate_ref, out_ref, *, row):
    total = jnp.dot(a0[...], w0[...], preferred_element_type=f32)
    for a, w in ((a1, w1), (a2, w2), (a3, w3)):
        total += jnp.dot(a[...], w[...], preferred_element_type=f32)
    out_ref[...] = (mixed_ref[...] + gate_ref[row : row + 1, :] * total).astype(bf16)


def output(where, attended, w_out, mixed, mod, row):
    tiles = 4
    width = D // tiles

    def weight(k):
        return pl.BlockSpec((WIDE, width), lambda i, p: ((p[0] + k) % RING, i))

    def body(*refs):
        output_kernel(*refs, row=row)

    return pl.pallas_call(
        body,
        grid_spec=pltpu.PrefetchScalarGridSpec(
            num_scalar_prefetch=1,
            grid=(tiles,),
            in_specs=[pl.BlockSpec((SLAB, WIDE), lambda i, p: (0, 0))] * 4
            + [weight(k) for k in range(RING)]
            + [
                pl.BlockSpec((SLAB, width), lambda i, p: (0, i)),
                pl.BlockSpec((8, width), lambda i, p: (0, 2 * tiles + i)),
            ],
            out_specs=pl.BlockSpec((SLAB, width), lambda i, p: (0, i)),
        ),
        out_shape=jax.ShapeDtypeStruct((SLAB, D), bf16),
        compiler_params=params(),
        name="output",
    )(where, *attended, w_out, w_out, w_out, w_out, mixed, mod)


def sent_round(blocks):
    return [blocks[0]] + [lax.ppermute(blocks[k], "patch", ring(k)) for k in range(1, RING)]


def sent_back(blocks):
    return [blocks[0]] + [
        lax.ppermute(blocks[k], "patch", ring(RING - k)) for k in range(1, RING)
    ]


def spread(own):
    other_y = lax.ppermute(own, "patch", ACROSS)
    other_core = lax.ppermute(own, "patch", CORE)
    return [own, other_core, other_y, lax.ppermute(other_y, "patch", CORE)]


def live_bias(counts, y, z, c):
    back = jnp.arange(RING, dtype=jnp.int32)
    chips = 2 * ((z - back) % RING)
    slabs = jnp.stack(
        [8 * yy + chips + cc for yy, cc in ((y, c), (y, 1 - c), (1 - y, c), (1 - y, 1 - c))]
    )
    live = jnp.arange(SLAB, dtype=jnp.int32) < counts[slabs][:, :, None]
    return jnp.where(live, 0.0, masked_score).astype(f32).reshape(4, RING * SLAB)


def shards(latent, stale_kv, timesteps, counts, conv_weight, w_mod, w_qkv, q_gain, k_gain, w_out):
    own_slab = lax.axis_index("patch")
    y, z, c = own_slab // 8, (own_slab // 2) % RING, own_slab % 2
    where = jnp.stack([z, c]).astype(jnp.int32)
    state = latent
    olds = None
    mod = modulation(timesteps, w_mod)
    bias = live_bias(counts, y, z, c)
    cache = None
    for step in range(STEPS):
        to_core = lax.dynamic_slice_in_dim(state, jnp.where(c == 0, SLAB - FRAME, 0), FRAME, 0)
        to_chip = lax.dynamic_slice_in_dim(state, jnp.where(c == 0, 0, SLAB - FRAME), FRAME, 0)
        core_rows = lax.ppermute(to_core, "patch", CORE)
        chip_rows = lax.ppermute(to_chip, "patch", NEXT_CHIP)
        if step == 0:
            old_blocks = sent_round(split_cache(where, stale_kv))
            olds = spread(jnp.concatenate(old_blocks, 0))
        *blocks, cache, mixed = project(
            where, state, core_rows, chip_rows, conv_weight, mod, q_gain, k_gain, w_qkv, step
        )
        fresh = sent_round(blocks)
        attended = attend(fresh, olds, bias)
        if step + 1 < STEPS:
            olds = spread(jnp.concatenate([block[:, WIDE:] for block in fresh], 0))
        state = output(where, sent_back(attended), w_out, mixed, mod, step)
    return (state, cache)


def solution(mesh):
    rows = P(("req", "patch"), None)
    return jax.shard_map(
        shards,
        mesh=mesh,
        in_specs=(rows, rows, P("req"), P("req"), P(), P(), P(), P(), P(), P()),
        out_specs=(rows, rows),
        check_vma=False,
    )
```

```python
import functools
import math

import jax
import jax.numpy as jnp
from jax import lax
from jax.experimental import pallas as pl
from jax.experimental.pallas import tpu as pltpu
from jax.sharding import PartitionSpec as P

HEAD = 128
FREQ = 256
FRAME = 80
STEPS = 2
SLAB = 128
D = 1536
GROUP = 3
WIDE = GROUP * HEAD
RING = 4
LOG2E = math.log2(math.e)

epsilon = 1e-06
masked_score = -1e30
f32 = jnp.float32
bf16 = jnp.bfloat16


def place(y, z, c):
    return 8 * y + 2 * z + c


DEVICES = [(y, z, c) for y in range(2) for z in range(RING) for c in range(2)]
CORE = [(place(y, z, c), place(y, z, 1 - c)) for y, z, c in DEVICES]
ACROSS = [(place(y, z, c), place(1 - y, z, c)) for y, z, c in DEVICES]


def ring(k):
    return [(place(y, z, c), place(y, (z + k) % RING, c)) for y, z, c in DEVICES]


NEXT_CHIP = [(p, p + 1) for p in range(1, 15, 2)] + [(p + 1, p) for p in range(1, 15, 2)]


VMEM = pl.BlockSpec(memory_space=pltpu.VMEM)
SMEM = pl.BlockSpec(memory_space=pltpu.SMEM)
ANY = pl.BlockSpec(memory_space=pl.ANY)
HBM = pl.BlockSpec(memory_space=pltpu.HBM)


def cost(microseconds):
    return pl.CostEstimate(
        flops=int(microseconds * 1e9), bytes_accessed=int(microseconds * 3e6), transcendentals=0
    )


KEPT = "kept"


def in_vmem(array):
    return pltpu.with_memory_space_constraint(array, pltpu.VMEM)


def in_hbm(array):
    return pltpu.with_memory_space_constraint(array, pltpu.HBM)


def call(body, name, microseconds, in_specs, outs, scratch=(), aliases=None, megabytes=12):
    return pl.pallas_call(
        body,
        in_specs=in_specs,
        out_specs=[VMEM if spec is KEPT else spec for _, _, spec in outs],
        out_shape=[
            (pltpu.VMEM if spec is KEPT else jax.ShapeDtypeStruct)(shape, dtype)
            for shape, dtype, spec in outs
        ],
        scratch_shapes=list(scratch),
        input_output_aliases=aliases or {},
        compiler_params=pltpu.CompilerParams(vmem_limit_bytes=megabytes * 2**20),
        cost_estimate=cost(microseconds),
        name=name,
    )


def edge_starts(core):
    last = SLAB - FRAME
    return (
        pl.multiple_of(jnp.where(core == 0, last, 0), 16),
        pl.multiple_of(jnp.where(core == 0, 0, last), 16),
    )


def prepare_kernel(place_ref, latent_ref, stale_ref, core_ref, chip_ref, o0, o1, o2, o3, sems):
    outs = (o0, o1, o2, o3)
    core_start, chip_start = edge_starts(place_ref[1])
    copies = [
        pltpu.make_async_copy(latent_ref.at[pl.ds(chip_start, FRAME), :], chip_ref, sems.at[8]),
        pltpu.make_async_copy(latent_ref.at[pl.ds(core_start, FRAME), :], core_ref, sems.at[9]),
    ]
    for k in range(RING):
        start = (place_ref[0] + k) % RING * WIDE
        for part in range(2):
            columns = pl.ds(pl.multiple_of(start + part * D, HEAD), WIDE)
            copies.append(
                pltpu.make_async_copy(
                    stale_ref.at[:, columns],
                    outs[k].at[:, part * WIDE : (part + 1) * WIDE],
                    sems.at[2 * k + part],
                )
            )
    for copy in copies:
        copy.start()
    for copy in copies:
        copy.wait()


def prepare(where, latent, stale_kv):
    edge = ((FRAME, D), bf16, VMEM)
    return call(
        prepare_kernel,
        "prepare",
        1,
        [SMEM, HBM, HBM],
        [edge, edge] + [((SLAB, 2 * WIDE), bf16, VMEM)] * RING,
        [pltpu.SemaphoreType.DMA((10,))],
    )(where, in_hbm(latent), in_hbm(stale_kv))


def mix_rows(place_ref, state_ref, core_ref, chip_ref, conv_ref, mod_ref, mixed_ref, normed_ref, row):
    first = place_ref[1] == 0
    state = state_ref[...].astype(f32)
    core_rows = core_ref[...].astype(f32)
    chip_rows = chip_ref[...].astype(f32)
    above = jnp.where(first, chip_rows, core_rows)
    below = jnp.where(first, core_rows, chip_rows)
    before = jnp.concatenate([above, state[: SLAB - FRAME]], 0)
    after_rows = jnp.concatenate([state[FRAME:], below], 0)
    mixed = (
        state
        + conv_ref[0:1, :] * before
        + conv_ref[1:2, :] * state
        + conv_ref[2:3, :] * after_rows
    )
    mixed_ref[...] = mixed
    shift = mod_ref[row : row + 1, :D]
    scale = mod_ref[row : row + 1, D : 2 * D]
    centred = mixed - jnp.mean(mixed, -1, keepdims=True)
    variance = jnp.mean(centred * centred, -1, keepdims=True)
    normed_ref[...] = (centred * lax.rsqrt(variance + epsilon) * (1.0 + scale) + shift).astype(bf16)


def embedding(moment):
    halfway = FREQ // 2
    index = lax.broadcasted_iota(jnp.int32, (halfway, 1), 0).astype(f32)
    angles = moment.astype(f32) * jnp.exp(-math.log(10000.0) * index / halfway)
    values = jnp.concatenate([jnp.cos(angles), jnp.sin(angles)], 0)
    return values / (1.0 + jnp.exp(-values))


def head_normed(block, gain):
    mean_square = jnp.mean(block * block, -1, keepdims=True)
    return (block * lax.rsqrt(mean_square + epsilon) * gain).astype(bf16)


def project_rows(normed, gain_ref, group, weights, out_ref):
    for part in range(3):
        block = jnp.dot(normed, weights[part], preferred_element_type=f32)
        if part < 2:
            gain = gain_ref[part : part + 1, pl.ds(group, WIDE)]
            for h in range(GROUP):
                here = slice(h * HEAD, (h + 1) * HEAD)
                out_ref[:, part * WIDE + h * HEAD : part * WIDE + (h + 1) * HEAD] = head_normed(
                    block[:, here], gain[:, here]
                )
        else:
            out_ref[:, part * WIDE :] = block.astype(bf16)


def open_kernel(
    place_ref, latent_ref, core_ref, chip_ref, taps_ref, q_gain_ref, k_gain_ref,
    w_mod_ref, w_qkv_ref, mod_ref, gains_ref, mixed_ref, o0, o1, o2, o3,
    mod_held, w_held, state_ref, conv_ref, normed_ref, sems
):
    outs = (o0, o1, o2, o3)
    tiles = mod_held.shape[0]
    tile = mod_held.shape[2]
    mods = [
        pltpu.make_async_copy(
            w_mod_ref.at[:, i * tile : (i + 1) * tile], mod_held.at[i], sems.at[i]
        )
        for i in range(tiles)
    ]
    rest = [
        pltpu.make_async_copy(latent_ref, state_ref, sems.at[tiles]),
        pltpu.make_async_copy(taps_ref, conv_ref, sems.at[tiles + 1]),
    ]
    groups, loads = {}, {}
    for k in range(RING):
        groups[k] = pl.multiple_of((place_ref[0] + k) % RING * WIDE, HEAD)
        loads[k] = [
            pltpu.make_async_copy(
                w_qkv_ref.at[:, pl.ds(pl.multiple_of(groups[k] + part * D, HEAD), WIDE)],
                w_held.at[3 * k + part],
                sems.at[tiles + 2 + 3 * k + part],
            )
            for part in range(3)
        ]
    for copy in (*rest, *mods, *loads[2]):
        copy.start()
    gains_ref[0:1, :] = (q_gain_ref[...] * (LOG2E / math.sqrt(HEAD))).reshape(1, D)
    gains_ref[1:2, :] = k_gain_ref[...].reshape(1, D)
    active = [embedding(place_ref[2 + s]) for s in range(STEPS)]
    for i, copy in enumerate(mods):
        copy.wait()
        if i == tiles // 2:
            for load in loads[1]:
                load.start()
        weights = mod_held[i]
        for s in range(STEPS):
            mod_ref[s : s + 1, i * tile : (i + 1) * tile] = jnp.sum(
                weights * active[s], 0, keepdims=True
            )
    for load in loads[3]:
        load.start()
    for copy in rest:
        copy.wait()
    mix_rows(place_ref, state_ref, core_ref, chip_ref, conv_ref, mod_ref, mixed_ref, normed_ref, 0)
    for k in (2, 1, 3, 0):
        if k == 2:
            for load in loads[0]:
                load.start()
        for load in loads[k]:
            load.wait()
        project_rows(
            normed_ref[...], gains_ref, groups[k], [w_held[3 * k + part] for part in range(3)], outs[k]
        )


def opening(where, state, core_rows, chip_rows, conv_weight, q_gain, k_gain, w_mod, w_qkv):
    tiles = 6
    return call(
        open_kernel,
        "opening",
        8,
        [SMEM, HBM, VMEM, VMEM, HBM, VMEM, VMEM, HBM, HBM],
        [((STEPS, w_mod.shape[1]), f32, VMEM), ((2, D), f32, VMEM), ((SLAB, D), f32, VMEM)]
        + [((SLAB, 3 * WIDE), bf16, VMEM)] * RING,
        [
            pltpu.VMEM((tiles, FREQ, w_mod.shape[1] // tiles), f32),
            pltpu.VMEM((3 * RING, D, WIDE), bf16),
            pltpu.VMEM((SLAB, D), bf16),
            pltpu.VMEM((3, D), f32),
            pltpu.VMEM((SLAB, D), bf16),
            pltpu.SemaphoreType.DMA((tiles + 2 + 3 * RING,)),
        ],
        megabytes=32,
    )(
        where, in_hbm(state), core_rows, chip_rows, in_hbm(conv_weight), q_gain, k_gain,
        in_hbm(w_mod), in_hbm(w_qkv),
    )


def mix_kernel(*refs, row):
    mix_rows(*refs, row)


def mix(where, state, core_rows, chip_rows, conv_weight, mod, row):
    return call(
        functools.partial(mix_kernel, row=row),
        "mix",
        1.2,
        [SMEM] + [VMEM] * 5,
        [((SLAB, D), f32, VMEM), ((SLAB, D), bf16, VMEM)],
    )(where, state, core_rows, chip_rows, conv_weight, mod)


def project_kernel(place_ref, normed_ref, gain_ref, w_ref, token_ref, out_ref, *, k):
    group = pl.multiple_of((place_ref[0] + k) % RING * WIDE, HEAD)
    weights = [
        w_ref[:, pl.ds(pl.multiple_of(group + part * D, HEAD), WIDE)] for part in range(3)
    ]
    project_rows(normed_ref[...], gain_ref, group, weights, out_ref)


def project(where, normed, gains, w_qkv, k, token):
    return call(
        functools.partial(project_kernel, k=k),
        "project",
        1.4,
        [SMEM] + [VMEM] * 3 + [ANY],
        [((SLAB, 3 * WIDE), bf16, VMEM)],
    )(where, normed, gains, w_qkv, token)[0]


def hold_kernel(*refs):
    pass


def held(array, tokens):
    return call(
        hold_kernel,
        "hold",
        0.1,
        [ANY] * (1 + len(tokens)),
        [(array.shape, array.dtype, ANY)],
        aliases={0: 0},
    )(array, *tokens)[0]


def stack_kernel(*refs):
    blocks, out_ref = refs[:RING], refs[-1]
    first = blocks[0].shape[1] - 2 * WIDE
    for k in range(RING):
        out_ref[k * SLAB : (k + 1) * SLAB, :] = blocks[k][:, first:]


def stack(blocks, token):
    return call(
        stack_kernel,
        "stack",
        1,
        [VMEM] * RING + [ANY],
        [((RING * SLAB, 2 * WIDE), bf16, VMEM)],
    )(*[blocks[k] for k in range(RING)], token)[0]


def join_kernel(place_ref, *refs):
    cache_ref = refs[-1]
    for k in range(RING):
        start = pl.multiple_of((place_ref[0] + k) % RING * WIDE, HEAD)
        cache_ref[:, pl.ds(start, WIDE)] = refs[k][:, WIDE : 2 * WIDE]
        cache_ref[:, pl.ds(pl.multiple_of(start + D, HEAD), WIDE)] = refs[k][:, 2 * WIDE :]


def join_cache(where, blocks, token):
    return call(
        join_kernel,
        "join_cache",
        1,
        [SMEM] + [VMEM] * RING + [ANY],
        [((SLAB, 2 * D), bf16, VMEM)],
    )(where, *[blocks[k] for k in range(RING)], token)[0]


def live_bias(place_ref, counts_ref):
    z, y, c = place_ref[0], place_ref[4], place_ref[1]
    index = lax.broadcasted_iota(jnp.int32, (1, SLAB), 1)
    rows = []
    for yy, cc in ((y, c), (y, 1 - c), (1 - y, c), (1 - y, 1 - c)):
        slabs = [8 * yy + 2 * ((z + RING - j) % RING) + cc for j in range(RING)]
        rows.append(
            jnp.concatenate(
                [jnp.where(index < counts_ref[slab], 0.0, masked_score) for slab in slabs], 1
            )
        )
    return rows


def attend_kernel(place_ref, counts_ref, *refs, slots, loads):
    n = len(slots)
    fresh, olds, outs = refs[:n], refs[n : n + 4], refs[n + 5 + loads :][:n]
    bias = live_bias(place_ref, counts_ref)
    if loads:
        load = pltpu.make_async_copy(refs[n + 5], refs[2 * n + 6], refs[2 * n + 7])
        load.start()
    rows = RING * SLAB
    ones = jnp.ones((rows, HEAD), bf16)

    def columns(part, h):
        return slice((part * GROUP + h) * HEAD, (part * GROUP + h + 1) * HEAD)

    for h in range(GROUP):
        for i, slot in enumerate(slots):
            queries = fresh[i][:, columns(0, h)]
            keys, values = [], []
            for a in range(4):
                for held, part in ((keys, 0), (values, 1)):
                    block = olds[a][:, columns(part, h)]
                    if a == 0:
                        pieces = [block[j * SLAB : (j + 1) * SLAB] for j in range(RING)]
                        pieces[slot] = fresh[i][:, columns(part + 1, h)]
                        block = jnp.concatenate(pieces, 0)
                    held.append(block)
            scores = [
                lax.dot_general(
                    queries, keys[a], (((1,), (1,)), ((), ())), preferred_element_type=f32
                )
                + bias[a]
                for a in range(4)
            ]
            highest = functools.reduce(
                jnp.maximum, [jnp.max(block, -1, keepdims=True) for block in scores]
            )
            summed = 0.0
            for a in range(4):
                probs = jnp.exp2(scores[a] - highest).astype(bf16)
                summed += jnp.dot(
                    probs, jnp.concatenate([values[a], ones], 1), preferred_element_type=f32
                )
            outs[i][:, columns(0, h)] = (summed[:, :HEAD] / summed[:, HEAD:]).astype(bf16)
    if loads:
        load.wait()


def attend(where, counts, fresh, olds, slots, token, weight=None):
    n = len(slots)
    loads = 0 if weight is None else 1
    return call(
        functools.partial(attend_kernel, slots=slots, loads=loads),
        "attend",
        2.4,
        [SMEM] * 2 + [VMEM] * (n + 4) + [ANY] + [HBM] * loads,
        [((SLAB, WIDE), bf16, VMEM)] * n + ([(weight.shape, bf16, KEPT)] if loads else []),
        [pltpu.SemaphoreType.DMA] if loads else [],
    )(
        where, counts, *[fresh[slot] for slot in slots], *olds, token,
        *([in_hbm(weight)] if loads else []),
    )


def output_kernel(
    place_ref, a0, a1, a2, a3, w_ref, mixed_ref, mod_ref, out_ref, core_ref, chip_ref, *, row
):
    total = 0.0
    for k, block in enumerate((a0, a1, a2, a3)):
        start = pl.multiple_of((place_ref[0] + k) % RING * WIDE, HEAD)
        total += jnp.dot(block[...], w_ref[pl.ds(start, WIDE), :], preferred_element_type=f32)
    gate = mod_ref[row : row + 1, 2 * D :]
    out_ref[...] = (mixed_ref[...] + gate * total).astype(bf16)
    core_start, chip_start = edge_starts(place_ref[1])
    core_ref[...] = out_ref[pl.ds(core_start, FRAME), :]
    chip_ref[...] = out_ref[pl.ds(chip_start, FRAME), :]


def output(where, attended, w_out, mixed, mod, row):
    edge = ((FRAME, D), bf16, VMEM)
    return call(
        functools.partial(output_kernel, row=row),
        "output",
        2,
        [SMEM] + [VMEM] * 7,
        [((SLAB, D), bf16, VMEM), edge, edge],
    )(where, *[attended[k] for k in range(RING)], in_vmem(w_out), mixed, mod)


def sent(block, k):
    return lax.ppermute(block, "patch", ring(k % RING)) if k % RING else block


def shards(latent, stale_kv, timesteps, counts, conv_weight, w_mod, w_qkv, q_gain, k_gain, w_out):
    own_slab = lax.axis_index("patch")
    y, z, c = own_slab // 8, (own_slab // 2) % RING, own_slab % 2
    where = jnp.stack([z, c, timesteps[0], timesteps[1], y]).astype(jnp.int32)
    state = latent
    to_core, to_chip, *pieces = prepare(where, latent, stale_kv)
    for step in range(STEPS):
        last = step + 1 == STEPS
        chip_rows = lax.ppermute(to_chip, "patch", NEXT_CHIP)
        core_rows = lax.ppermute(to_core, "patch", CORE)
        if step == 0:
            arrived = {k: sent(pieces[k], k) for k in (2, 1, 3, 0)}
            mod, gains, mixed, *blocks = opening(
                where, state, core_rows, chip_rows, conv_weight, q_gain, k_gain, w_mod, w_qkv
            )
            old = stack(arrived, blocks[2])
            old_y = lax.ppermute(old, "patch", ACROSS)
            old_core = lax.ppermute(old, "patch", CORE)
            fresh = {k: sent(blocks[k], k) for k in (2, 1, 3, 0)}
        else:
            mixed, normed = mix(where, state, core_rows, chip_rows, conv_weight, mod, step)
            blocks, fresh = {}, {}
            token = gains
            for k in (2, 1, 3):
                token = blocks[k] = project(where, normed, gains, w_qkv, k, token)
                fresh[k] = sent(token, k)
            blocks[0] = fresh[0] = project(where, normed, gains, w_qkv, 0, fresh[2])
        old_y = held(old_y, [fresh[k] for k in (2, 1, 3, 0)])
        olds = [old, old_core, old_y, lax.ppermute(old_y, "patch", CORE)]
        if step == 0:
            *far, w_out = attend(where, counts, fresh, olds, (2, 1), gains, w_out)
        else:
            far = attend(where, counts, fresh, olds, (2, 1), gains)
        returned = {2: sent(far[0], -2), 1: sent(far[1], -1)}
        near = attend(where, counts, fresh, olds, (3, 0), far[0])
        returned |= {3: sent(near[0], -3), 0: near[1]}
        if last:
            cache = join_cache(where, blocks, near[1])
        else:
            old = stack(fresh, returned[2])
            old_y = lax.ppermute(old, "patch", ACROSS)
            old_core = lax.ppermute(old, "patch", CORE)
        state, to_core, to_chip = output(where, returned, w_out, mixed, mod, step)
    return (state, cache)


def solution(mesh):
    rows = P(("req", "patch"), None)
    return jax.shard_map(
        shards,
        mesh=mesh,
        in_specs=(rows, rows, P("req"), P("req"), P(), P(), P(), P(), P(), P()),
        out_specs=(rows, rows),
        check_vma=False,
    )
```

```python
import functools
import math

import jax
import jax.numpy as jnp
from jax import lax
from jax.experimental import pallas as pl
from jax.experimental.pallas import tpu as pltpu
from jax.sharding import PartitionSpec as P

HEAD = 128
FREQ = 256
FRAME = 80
STEPS = 2
SLAB = 128
D = 1536
GROUP = 3
WIDE = GROUP * HEAD
RING = 4
LOG2E = math.log2(math.e)
ORDER = (2, 1, 3, 0)

epsilon = 1e-06
masked_score = -1e30
f32 = jnp.float32
bf16 = jnp.bfloat16


def place(y, z, c):
    return 8 * y + 2 * z + c


DEVICES = [(y, z, c) for y in range(2) for z in range(RING) for c in range(2)]
CORE = [(place(y, z, c), place(y, z, 1 - c)) for y, z, c in DEVICES]
ACROSS = [(place(y, z, c), place(1 - y, z, c)) for y, z, c in DEVICES]


def ring(k):
    return [(place(y, z, c), place(y, (z + k) % RING, c)) for y, z, c in DEVICES]


NEXT_CHIP = [(p, p + 1) for p in range(1, 15, 2)] + [(p + 1, p) for p in range(1, 15, 2)]


VMEM = pl.BlockSpec(memory_space=pltpu.VMEM)
SMEM = pl.BlockSpec(memory_space=pltpu.SMEM)
ANY = pl.BlockSpec(memory_space=pl.ANY)
HBM = pl.BlockSpec(memory_space=pltpu.HBM)


def cost(microseconds):
    return pl.CostEstimate(
        flops=int(microseconds * 1e9), bytes_accessed=int(microseconds * 1e6), transcendentals=0
    )


KEPT = "kept"


def in_vmem(array):
    return pltpu.with_memory_space_constraint(array, pltpu.VMEM)


def in_hbm(array):
    return pltpu.with_memory_space_constraint(array, pltpu.HBM)


def call(body, name, in_specs, outs, scratch=(), aliases=None, megabytes=12, us=0.1):
    return pl.pallas_call(
        body,
        in_specs=in_specs,
        out_specs=[VMEM if spec is KEPT else spec for _, _, spec in outs],
        out_shape=[
            (pltpu.VMEM if spec is KEPT else jax.ShapeDtypeStruct)(shape, dtype)
            for shape, dtype, spec in outs
        ],
        scratch_shapes=list(scratch),
        input_output_aliases=aliases or {},
        compiler_params=pltpu.CompilerParams(vmem_limit_bytes=megabytes * 2**20),
        cost_estimate=cost(us),
        name=name,
    )


def edge_starts(core):
    last = SLAB - FRAME
    return (
        pl.multiple_of(jnp.where(core == 0, last, 0), 16),
        pl.multiple_of(jnp.where(core == 0, 0, last), 16),
    )


def prepare_kernel(place_ref, latent_ref, stale_ref, core_ref, chip_ref, o0, o1, o2, o3, sems):
    outs = (o0, o1, o2, o3)
    core_start, chip_start = edge_starts(place_ref[1])
    copies = [
        pltpu.make_async_copy(latent_ref.at[pl.ds(chip_start, FRAME), :], chip_ref, sems.at[8]),
        pltpu.make_async_copy(latent_ref.at[pl.ds(core_start, FRAME), :], core_ref, sems.at[9]),
    ]
    for k in range(RING):
        start = (place_ref[0] + k) % RING * WIDE
        for part in range(2):
            columns = pl.ds(pl.multiple_of(start + part * D, HEAD), WIDE)
            copies.append(
                pltpu.make_async_copy(
                    stale_ref.at[:, columns],
                    outs[k].at[:, part * WIDE : (part + 1) * WIDE],
                    sems.at[2 * k + part],
                )
            )
    for copy in copies:
        copy.start()
    for copy in copies:
        copy.wait()


def prepare(where, latent, stale_kv):
    edge = ((FRAME, D), bf16, VMEM)
    return call(
        prepare_kernel,
        "prepare",
        [SMEM, HBM, HBM],
        [edge, edge] + [((SLAB, 2 * WIDE), bf16, VMEM)] * RING,
        [pltpu.SemaphoreType.DMA((10,))],
    )(where, in_hbm(latent), in_hbm(stale_kv))


def mix_rows(place_ref, state_ref, core_ref, chip_ref, conv_ref, mod_ref, mixed_ref, normed_ref, row):
    first = place_ref[1] == 0
    state = state_ref[...].astype(f32)
    core_rows = core_ref[...].astype(f32)
    chip_rows = chip_ref[...].astype(f32)
    above = jnp.where(first, chip_rows, core_rows)
    below = jnp.where(first, core_rows, chip_rows)
    before = jnp.concatenate([above, state[: SLAB - FRAME]], 0)
    after_rows = jnp.concatenate([state[FRAME:], below], 0)
    mixed = (
        state
        + conv_ref[0:1, :] * before
        + conv_ref[1:2, :] * state
        + conv_ref[2:3, :] * after_rows
    )
    mixed_ref[...] = mixed
    shift = mod_ref[row : row + 1, :D]
    scale = mod_ref[row : row + 1, D : 2 * D]
    centred = mixed - jnp.mean(mixed, -1, keepdims=True)
    variance = jnp.mean(centred * centred, -1, keepdims=True)
    normed_ref[...] = (centred * lax.rsqrt(variance + epsilon) * (1.0 + scale) + shift).astype(bf16)


def embedding(moment):
    halfway = FREQ // 2
    index = lax.broadcasted_iota(jnp.int32, (halfway, 1), 0).astype(f32)
    angles = moment.astype(f32) * jnp.exp(-math.log(10000.0) * index / halfway)
    values = jnp.concatenate([jnp.cos(angles), jnp.sin(angles)], 0)
    return values / (1.0 + jnp.exp(-values))


def head_normed(block, gain):
    mean_square = jnp.mean(block * block, -1, keepdims=True)
    return (block * lax.rsqrt(mean_square + epsilon) * gain).astype(bf16)


def normed_heads(normed, weight, gain_ref, row, group, out_ref, start):
    block = jnp.dot(normed, weight, preferred_element_type=f32)
    gain = gain_ref[row : row + 1, pl.ds(group, WIDE)]
    for h in range(GROUP):
        here = slice(h * HEAD, (h + 1) * HEAD)
        out_ref[:, start + h * HEAD : start + (h + 1) * HEAD] = head_normed(
            block[:, here], gain[:, here]
        )


def group_start(place_ref, k):
    return pl.multiple_of((place_ref[0] + k) % RING * WIDE, HEAD)


def weight_copies(place_ref, w_ref, held, sems, parts):
    copies = {}
    for k in range(RING):
        copies[k] = []
        for i, part in enumerate(parts):
            columns = pl.ds(pl.multiple_of(group_start(place_ref, k) + part * D, HEAD), WIDE)
            slot = k * len(parts) + i
            copies[k].append(
                pltpu.make_async_copy(w_ref.at[:, columns], held.at[slot], sems.at[slot])
            )
    return copies


def project_queries(place_ref, normed_ref, gains_ref, copies, held, outs):
    for k in ORDER:
        for copy in copies[k]:
            copy.wait()
        normed_heads(
            normed_ref[...], held[k], gains_ref, 0, group_start(place_ref, k), outs[k], 0
        )


def fill_bias(place_ref, counts_ref, bias_ref):
    z, c, y = place_ref[0], place_ref[1], place_ref[4]
    index = lax.broadcasted_iota(jnp.int32, (1, SLAB), 1)
    for a, (yy, cc) in enumerate(((y, c), (y, 1 - c), (1 - y, c), (1 - y, 1 - c))):
        for j in range(RING):
            slab = 8 * yy + 2 * ((z + RING - j) % RING) + cc
            here = slice(j * SLAB, (j + 1) * SLAB)
            row = jnp.where(index < counts_ref[slab], 0.0, masked_score)
            bias_ref[a : a + 1, here] = row
            if a == 0:
                for slot in range(RING):
                    bias_ref[4 + slot : 5 + slot, here] = (
                        jnp.full((1, SLAB), masked_score, f32) if slot == j else row
                    )
                if j == 0:
                    bias_ref[8:9, here] = row


def open_kernel(
    place_ref, counts_ref, latent_ref, core_ref, chip_ref, taps_ref, q_gain_ref, k_gain_ref,
    w_mod_ref, w_qkv_ref, mod_ref, gains_ref, bias_ref, mixed_ref, o0, o1, o2, o3,
    mod_held, w_held, state_ref, conv_ref, q_held, k_held, normed_ref, sems, w_sems
):
    outs = (o0, o1, o2, o3)
    tiles = mod_held.shape[0]
    tile = mod_held.shape[2]
    mods = [
        pltpu.make_async_copy(
            w_mod_ref.at[:, i * tile : (i + 1) * tile], mod_held.at[i], sems.at[i]
        )
        for i in range(tiles)
    ]
    rest = [
        pltpu.make_async_copy(latent_ref, state_ref, sems.at[tiles]),
        pltpu.make_async_copy(taps_ref, conv_ref, sems.at[tiles + 1]),
        pltpu.make_async_copy(q_gain_ref, q_held, sems.at[tiles + 2]),
        pltpu.make_async_copy(k_gain_ref, k_held, sems.at[tiles + 3]),
    ]
    loads = weight_copies(place_ref, w_qkv_ref, w_held, w_sems, (0, 1, 2))
    for copy in (*rest, *mods, *loads[ORDER[0]]):
        copy.start()
    active = [embedding(place_ref[2 + s]) for s in range(STEPS)]
    fill_bias(place_ref, counts_ref, bias_ref)
    for copy in rest:
        copy.wait()
    gains_ref[0:1, :] = (q_held[...] * (LOG2E / math.sqrt(HEAD))).reshape(1, D)
    gains_ref[1:2, :] = k_held[...].reshape(1, D)
    for i, copy in enumerate(mods):
        copy.wait()
        if i == tiles // 2:
            for load in loads[ORDER[1]]:
                load.start()
        weights = mod_held[i]
        for s in range(STEPS):
            mod_ref[s : s + 1, i * tile : (i + 1) * tile] = jnp.sum(
                weights * active[s], 0, keepdims=True
            )
    for k in ORDER[2:]:
        for load in loads[k]:
            load.start()
    mix_rows(place_ref, state_ref, core_ref, chip_ref, conv_ref, mod_ref, mixed_ref, normed_ref, 0)
    for k in ORDER:
        for load in loads[k]:
            load.wait()
        group = group_start(place_ref, k)
        for part in range(2):
            normed_heads(
                normed_ref[...], w_held[3 * k + part], gains_ref, part, group, outs[k], part * WIDE
            )
        outs[k][:, 2 * WIDE :] = jnp.dot(
            normed_ref[...], w_held[3 * k + 2], preferred_element_type=f32
        ).astype(bf16)


def opening(where, counts, state, core_rows, chip_rows, conv_weight, q_gain, k_gain, w_mod, w_qkv):
    tiles = 6
    return call(
        open_kernel,
        "opening",
        [SMEM, SMEM, HBM, VMEM, VMEM] + [HBM] * 5,
        [
            ((STEPS, w_mod.shape[1]), f32, VMEM),
            ((2, D), f32, VMEM),
            ((16, RING * SLAB), f32, VMEM),
            ((SLAB, D), f32, VMEM),
        ]
        + [((SLAB, 3 * WIDE), bf16, VMEM)] * RING,
        [
            pltpu.VMEM((tiles, FREQ, w_mod.shape[1] // tiles), f32),
            pltpu.VMEM((3 * RING, D, WIDE), bf16),
            pltpu.VMEM((SLAB, D), bf16),
            pltpu.VMEM((3, D), f32),
            pltpu.VMEM((D,), f32),
            pltpu.VMEM((D,), f32),
            pltpu.VMEM((SLAB, D), bf16),
            pltpu.SemaphoreType.DMA((tiles + 4,)),
            pltpu.SemaphoreType.DMA((3 * RING,)),
        ],
        megabytes=32,
    )(
        where, counts, in_hbm(state), core_rows, chip_rows, in_hbm(conv_weight), in_hbm(q_gain),
        in_hbm(k_gain), in_hbm(w_mod), in_hbm(w_qkv),
    )


def next_kernel(
    place_ref, state_ref, core_ref, chip_ref, conv_ref, mod_ref, gains_ref, w_qkv_ref,
    mixed_ref, normed_ref, o0, o1, o2, o3, w_held, w_sems, *, row
):
    loads = weight_copies(place_ref, w_qkv_ref, w_held, w_sems, (0,))
    for k in ORDER:
        for copy in loads[k]:
            copy.start()
    mix_rows(
        place_ref, state_ref, core_ref, chip_ref, conv_ref, mod_ref, mixed_ref, normed_ref, row
    )
    project_queries(place_ref, normed_ref, gains_ref, loads, w_held, (o0, o1, o2, o3))


def next_queries(where, state, core_rows, chip_rows, conv_weight, mod, gains, w_qkv, row):
    return call(
        functools.partial(next_kernel, row=row),
        "next_queries",
        [SMEM] + [VMEM] * 6 + [HBM],
        [((SLAB, D), f32, VMEM), ((SLAB, D), bf16, VMEM)] + [((SLAB, WIDE), bf16, VMEM)] * RING,
        [pltpu.VMEM((RING, D, WIDE), bf16), pltpu.SemaphoreType.DMA((RING,))],
    )(where, state, core_rows, chip_rows, conv_weight, mod, gains, in_hbm(w_qkv))


def dots(queries, keys):
    return lax.dot_general(queries, keys, (((1,), (1,)), ((), ())), preferred_element_type=f32)


def home_kernel(bias_ref, *refs):
    queries, keys, values = refs[:RING], refs[RING : 2 * RING], refs[2 * RING : 3 * RING]
    summed_ref, lse_ref = refs[-2:]
    bias = bias_ref[8:9, :SLAB]
    lanes = lax.broadcasted_iota(jnp.int32, (SLAB, HEAD), 1)
    ones = jnp.ones((SLAB, HEAD), bf16)
    heads = [slice(h * HEAD, (h + 1) * HEAD) for h in range(GROUP)]
    for pair in ((0, 1), (2, 3)):
        places = [(k, here) for k in pair for here in heads]
        first = keys[0].shape[1] - 2 * WIDE
        scores = [
            dots(queries[k][:, here], keys[k][:, first + here.start : first + here.stop]) + bias
            for k, here in places
        ]
        highest = [jnp.max(block, -1, keepdims=True) for block in scores]
        probs = [jnp.exp2(block - top).astype(bf16) for block, top in zip(scores, highest)]
        start = values[0].shape[1] - WIDE
        both = [
            jnp.dot(
                block,
                jnp.concatenate([values[k][:, start + here.start : start + here.stop], ones], 1),
                preferred_element_type=f32,
            )
            for block, (k, here) in zip(probs, places)
        ]
        for block, (k, here) in zip(both, places):
            summed_ref[:, k * WIDE + here.start : k * WIDE + here.stop] = (
                block[:, :HEAD] / block[:, HEAD:]
            )
        for i, k in enumerate(pair):
            lse = jnp.zeros((SLAB, HEAD), f32)
            for h in range(GROUP):
                n = i * GROUP + h
                lse = jnp.where(lanes == h, highest[n] + jnp.log2(both[n][:, HEAD:]), lse)
            lse_ref[:, k * HEAD : (k + 1) * HEAD] = lse


def at_home(bias, queries, keys, values, token):
    return call(
        home_kernel,
        "at_home",
        [VMEM] * (3 * RING + 1) + [ANY],
        [((SLAB, D), f32, VMEM), ((SLAB, RING * HEAD), f32, VMEM)],
    )(bias, *queries, *keys, *values, token)


def last_keys_kernel(
    place_ref, normed_ref, gains_ref, w_ref, token_ref, o0, o1, o2, o3, cache_ref, w_held, w_sems
):
    outs = (o0, o1, o2, o3)
    loads = weight_copies(place_ref, w_ref, w_held, w_sems, (1, 2))
    for k in ORDER:
        for copy in loads[k]:
            copy.start()
    for k in ORDER:
        for copy in loads[k]:
            copy.wait()
        group = group_start(place_ref, k)
        normed_heads(normed_ref[...], w_held[2 * k], gains_ref, 1, group, outs[k], 0)
        values = jnp.dot(
            normed_ref[...], w_held[2 * k + 1], preferred_element_type=f32
        ).astype(bf16)
        outs[k][:, WIDE:] = values
        cache_ref[:, pl.ds(group, WIDE)] = outs[k][:, :WIDE]
        cache_ref[:, pl.ds(pl.multiple_of(group + D, HEAD), WIDE)] = values


def last_keys(where, normed, gains, w_qkv, token):
    return call(
        last_keys_kernel,
        "last_keys",
        [SMEM] + [VMEM] * 2 + [HBM, ANY],
        [((SLAB, 2 * WIDE), bf16, VMEM)] * RING + [((SLAB, 2 * D), bf16, VMEM)],
        [pltpu.VMEM((2 * RING, D, WIDE), bf16), pltpu.SemaphoreType.DMA((2 * RING,))],
        megabytes=24,
    )(where, normed, gains, in_hbm(w_qkv), token)


def hold_kernel(*refs):
    pass


def held(array, tokens):
    return call(
        hold_kernel,
        "hold",
        [ANY] * (1 + len(tokens)),
        [(array.shape, array.dtype, ANY)],
        aliases={0: 0},
    )(array, *tokens)[0]


def stack_kernel(*refs):
    blocks, out_ref = refs[:RING], refs[-1]
    first = blocks[0].shape[1] - 2 * WIDE
    for k in range(RING):
        out_ref[k * SLAB : (k + 1) * SLAB, :] = blocks[k][:, first:]


def stack(blocks, token):
    return call(
        stack_kernel,
        "stack",
        [VMEM] * RING + [ANY],
        [((RING * SLAB, 2 * WIDE), bf16, VMEM)],
    )(*[blocks[k] for k in range(RING)], token)[0]


def attend_kernel(q0, q1, q2, q3, a0, a1, a2, a3, bias_ref, token_ref, *outs):
    queries = (q0, q1, q2, q3)
    olds = (a0, a1, a2, a3)
    lanes = lax.broadcasted_iota(jnp.int32, (SLAB, HEAD), 1)
    ones = jnp.ones((RING * SLAB, HEAD), bf16)
    lse = [jnp.zeros((SLAB, HEAD), f32)] * RING
    for h in range(GROUP):
        here = slice(h * HEAD, (h + 1) * HEAD)
        there = slice(WIDE + h * HEAD, WIDE + (h + 1) * HEAD)
        keys = [old[:, here] for old in olds]
        values = [jnp.concatenate([old[:, there], ones], 1) for old in olds]
        for pair in ((0, 1), (2, 3)):
            joined = jnp.concatenate([queries[slot][:, here] for slot in pair], 0)
            products = [dots(joined, keys[a]) for a in range(4)]
            for i, slot in enumerate(pair):
                scores = []
                for a in range(4):
                    row = a if a else 4 + slot
                    scores.append(
                        products[a][i * SLAB : (i + 1) * SLAB] + bias_ref[row : row + 1, :]
                    )
                highest = functools.reduce(
                    jnp.maximum, [jnp.max(block, -1, keepdims=True) for block in scores]
                )
                both = 0.0
                for a in range(4):
                    probs = jnp.exp2(scores[a] - highest).astype(bf16)
                    both += jnp.dot(probs, values[a], preferred_element_type=f32)
                total = both[:, HEAD:]
                outs[slot][:, here] = (both[:, :HEAD] / total).astype(bf16)
                lse[slot] = jnp.where(lanes == h, highest + jnp.log2(total), lse[slot])
    for slot in range(RING):
        rest = lse[slot]
        packed = 0.0
        for part in range(3):
            piece = rest.astype(bf16).astype(f32)
            rest = rest - piece
            packed += pltpu.roll(piece, part * GROUP, 1) if part else piece
        outs[slot][:, WIDE:] = packed.astype(bf16)


def attend(queries, olds, bias, token):
    return call(
        attend_kernel,
        "attend",
        [VMEM] * 9 + [ANY],
        [((SLAB, WIDE + HEAD), bf16, VMEM)] * RING,
        us=6,
    )(*[queries[k] for k in range(RING)], *olds, bias, token)


def output_kernel(
    place_ref, a0, a1, a2, a3, w_ref, summed_ref, lse_ref, mixed_ref, mod_ref,
    out_ref, core_ref, chip_ref, *, row
):
    total = 0.0
    for k, away in enumerate((a0, a1, a2, a3)):
        pieces = away[:, WIDE:].astype(f32)
        lse = (
            pieces
            + pltpu.roll(pieces, HEAD - GROUP, 1)
            + pltpu.roll(pieces, HEAD - 2 * GROUP, 1)
        )
        home = lse_ref[:, k * HEAD : (k + 1) * HEAD]
        share = 1.0 / (1.0 + jnp.exp2(home - lse))
        merged = []
        for h in range(GROUP):
            here = slice(k * WIDE + h * HEAD, k * WIDE + (h + 1) * HEAD)
            part = share[:, h : h + 1]
            merged.append(
                part * away[:, h * HEAD : (h + 1) * HEAD].astype(f32)
                + (1.0 - part) * summed_ref[:, here]
            )
        attended = jnp.concatenate(merged, 1).astype(bf16)
        start = group_start(place_ref, k)
        total += jnp.dot(attended, w_ref[pl.ds(start, WIDE), :], preferred_element_type=f32)
    gate = mod_ref[row : row + 1, 2 * D :]
    out_ref[...] = (mixed_ref[...] + gate * total).astype(bf16)
    core_start, chip_start = edge_starts(place_ref[1])
    core_ref[...] = out_ref[pl.ds(core_start, FRAME), :]
    chip_ref[...] = out_ref[pl.ds(chip_start, FRAME), :]


def output(where, away, summed, lse, w_out, mixed, mod, row):
    edge = ((FRAME, D), bf16, VMEM)
    return call(
        functools.partial(output_kernel, row=row),
        "output",
        [SMEM] + [VMEM] * 9,
        [((SLAB, D), bf16, VMEM), edge, edge],
    )(
        where, *[away[k] for k in range(RING)], w_out, summed, lse, mixed, mod
    )


def sent(block, k):
    return lax.ppermute(block, "patch", ring(k % RING)) if k % RING else block


def shards(latent, stale_kv, timesteps, counts, conv_weight, w_mod, w_qkv, q_gain, k_gain, w_out):
    own_slab = lax.axis_index("patch")
    y, z, c = own_slab // 8, (own_slab // 2) % RING, own_slab % 2
    where = jnp.stack([z, c, timesteps[0], timesteps[1], y]).astype(jnp.int32)
    to_core, to_chip, *pieces = prepare(where, latent, stale_kv)
    chip_rows = lax.ppermute(to_chip, "patch", NEXT_CHIP)
    core_rows = lax.ppermute(to_core, "patch", CORE)
    arrived = {k: sent(pieces[k], k) for k in ORDER}
    mod, gains, bias, mixed, *blocks = opening(
        where, counts, latent, core_rows, chip_rows, conv_weight, q_gain, k_gain, w_mod, w_qkv
    )
    old = stack(arrived, mixed)
    old_y = lax.ppermute(old, "patch", ACROSS)
    old_core = lax.ppermute(old, "patch", CORE)
    fresh = {k: sent(blocks[k], k) for k in ORDER}
    summed, lse = at_home(bias, blocks, blocks, blocks, old)
    new = stack(fresh, lse)
    new_y = lax.ppermute(new, "patch", ACROSS)
    new_core = lax.ppermute(new, "patch", CORE)
    old_y = held(old_y, [new])
    olds = [old, old_core, old_y, lax.ppermute(old_y, "patch", CORE)]
    found = attend(fresh, olds, bias, new)
    away = {k: sent(found[k], -k) for k in ORDER}
    state, to_core, to_chip = output(where, away, summed, lse, w_out, mixed, mod, 0)

    chip_rows = lax.ppermute(to_chip, "patch", NEXT_CHIP)
    core_rows = lax.ppermute(to_core, "patch", CORE)
    mixed, normed, *own = next_queries(
        where, state, core_rows, chip_rows, conv_weight, mod, gains, w_qkv, 1
    )
    queries = {k: sent(own[k], k) for k in ORDER}
    new_y = held(new_y, own[:1])
    olds = [new, new_core, new_y, lax.ppermute(new_y, "patch", CORE)]
    *pairs, cache = last_keys(where, normed, gains, w_qkv, normed)
    found = attend(queries, olds, bias, pairs[0])
    away = {k: sent(found[k], -k) for k in ORDER}
    summed, lse = at_home(bias, own, pairs, pairs, found[0])
    state, _, _ = output(where, away, summed, lse, w_out, mixed, mod, 1)
    return (state, cache)


def solution(mesh):
    rows = P(("req", "patch"), None)
    return jax.shard_map(
        shards,
        mesh=mesh,
        in_specs=(rows, rows, P("req"), P("req"), P(), P(), P(), P(), P(), P()),
        out_specs=(rows, rows),
        check_vma=False,
    )
```

```python
import functools
import math

import jax
import jax.numpy as jnp
from jax import lax
from jax.experimental import pallas as pl
from jax.experimental.pallas import tpu as pltpu
from jax.sharding import PartitionSpec as P

HEAD = 128
FREQ = 256
FRAME = 80
STEPS = 2
SLAB = 128
D = 1536
GROUP = 3
WIDE = GROUP * HEAD
RING = 4
LOG2E = math.log2(math.e)
ORDER = (2, 1, 3, 0)

epsilon = 1e-06
masked_score = -1e30
f32 = jnp.float32
bf16 = jnp.bfloat16


def place(y, z, c):
    return 8 * y + 2 * z + c


DEVICES = [(y, z, c) for y in range(2) for z in range(RING) for c in range(2)]
CORE = [(place(y, z, c), place(y, z, 1 - c)) for y, z, c in DEVICES]
ACROSS = [(place(y, z, c), place(1 - y, z, c)) for y, z, c in DEVICES]


def ring(k):
    return [(place(y, z, c), place(y, (z + k) % RING, c)) for y, z, c in DEVICES]


NEXT_CHIP = [(p, p + 1) for p in range(1, 15, 2)] + [(p + 1, p) for p in range(1, 15, 2)]


VMEM = pl.BlockSpec(memory_space=pltpu.VMEM)
SMEM = pl.BlockSpec(memory_space=pltpu.SMEM)
ANY = pl.BlockSpec(memory_space=pl.ANY)
HBM = pl.BlockSpec(memory_space=pltpu.HBM)


def cost(microseconds):
    return pl.CostEstimate(
        flops=int(microseconds * 1e9), bytes_accessed=int(microseconds * 1e6), transcendentals=0
    )


KEPT = "kept"


def in_vmem(array):
    return pltpu.with_memory_space_constraint(array, pltpu.VMEM)


def in_hbm(array):
    return pltpu.with_memory_space_constraint(array, pltpu.HBM)


def call(body, name, in_specs, outs, scratch=(), aliases=None, megabytes=10, us=0.1):
    return pl.pallas_call(
        body,
        in_specs=in_specs,
        out_specs=[VMEM if spec is KEPT else spec for _, _, spec in outs],
        out_shape=[
            (pltpu.VMEM if spec is KEPT else jax.ShapeDtypeStruct)(shape, dtype)
            for shape, dtype, spec in outs
        ],
        scratch_shapes=list(scratch),
        input_output_aliases=aliases or {},
        compiler_params=pltpu.CompilerParams(vmem_limit_bytes=megabytes * 2**20),
        cost_estimate=cost(us),
        name=name,
    )


def edge_starts(core):
    last = SLAB - FRAME
    return (
        pl.multiple_of(jnp.where(core == 0, last, 0), 16),
        pl.multiple_of(jnp.where(core == 0, 0, last), 16),
    )


def prepare_kernel(place_ref, latent_ref, stale_ref, core_ref, chip_ref, o0, o1, o2, o3, sems):
    outs = (o0, o1, o2, o3)
    core_start, chip_start = edge_starts(place_ref[1])
    copies = [
        pltpu.make_async_copy(latent_ref.at[pl.ds(chip_start, FRAME), :], chip_ref, sems.at[8]),
        pltpu.make_async_copy(latent_ref.at[pl.ds(core_start, FRAME), :], core_ref, sems.at[9]),
    ]
    for k in range(RING):
        start = (place_ref[0] + k) % RING * WIDE
        for part in range(2):
            columns = pl.ds(pl.multiple_of(start + part * D, HEAD), WIDE)
            copies.append(
                pltpu.make_async_copy(
                    stale_ref.at[:, columns],
                    outs[k].at[:, part * WIDE : (part + 1) * WIDE],
                    sems.at[2 * k + part],
                )
            )
    for copy in copies:
        copy.start()
    for copy in copies:
        copy.wait()


def prepare(where, latent, stale_kv):
    edge = ((FRAME, D), bf16, VMEM)
    return call(
        prepare_kernel,
        "prepare",
        [SMEM, HBM, HBM],
        [edge, edge] + [((SLAB, 2 * WIDE), bf16, VMEM)] * RING,
        [pltpu.SemaphoreType.DMA((10,))],
        us=8,
    )(where, in_hbm(latent), in_hbm(stale_kv))


def mix_rows(place_ref, state_ref, core_ref, chip_ref, conv_ref, mod_ref, mixed_ref, normed_ref, row):
    first = place_ref[1] == 0
    state = state_ref[...].astype(f32)
    core_rows = core_ref[...].astype(f32)
    chip_rows = chip_ref[...].astype(f32)
    above = jnp.where(first, chip_rows, core_rows)
    below = jnp.where(first, core_rows, chip_rows)
    before = jnp.concatenate([above, state[: SLAB - FRAME]], 0)
    after_rows = jnp.concatenate([state[FRAME:], below], 0)
    mixed = (
        state
        + conv_ref[0:1, :] * before
        + conv_ref[1:2, :] * state
        + conv_ref[2:3, :] * after_rows
    )
    mixed_ref[...] = mixed
    shift = mod_ref[row : row + 1, :D]
    scale = mod_ref[row : row + 1, D : 2 * D]
    centred = mixed - jnp.mean(mixed, -1, keepdims=True)
    variance = jnp.mean(centred * centred, -1, keepdims=True)
    normed_ref[...] = (centred * lax.rsqrt(variance + epsilon) * (1.0 + scale) + shift).astype(bf16)


def embedding(moment):
    halfway = FREQ // 2
    index = lax.broadcasted_iota(jnp.int32, (halfway, 1), 0).astype(f32)
    angles = moment.astype(f32) * jnp.exp(-math.log(10000.0) * index / halfway)
    values = jnp.concatenate([jnp.cos(angles), jnp.sin(angles)], 0)
    return values / (1.0 + jnp.exp(-values))


def head_normed(block, gain):
    mean_square = jnp.mean(block * block, -1, keepdims=True)
    return (block * lax.rsqrt(mean_square + epsilon) * gain).astype(bf16)


def normed_heads(normed, weight, gain_ref, row, group, out_ref, start):
    block = jnp.dot(normed, weight, preferred_element_type=f32)
    gain = gain_ref[row : row + 1, pl.ds(group, WIDE)]
    for h in range(GROUP):
        here = slice(h * HEAD, (h + 1) * HEAD)
        out_ref[:, start + h * HEAD : start + (h + 1) * HEAD] = head_normed(
            block[:, here], gain[:, here]
        )


def group_start(place_ref, k):
    return pl.multiple_of((place_ref[0] + k) % RING * WIDE, HEAD)


def project(normed, w_ref, gains_ref, part, held_ref, first):
    block = jnp.dot(normed, w_ref[:, part * D : (part + 1) * D], preferred_element_type=f32)
    if part == 2:
        held_ref[:, first : first + D] = block.astype(bf16)
        return
    for h in range(D // HEAD):
        here = slice(h * HEAD, (h + 1) * HEAD)
        held_ref[:, first + here.start : first + here.stop] = head_normed(
            block[:, here], gains_ref[part : part + 1, here]
        )


def dealt(place_ref, held_ref, parts, outs):
    for k, out_ref in enumerate(outs):
        for i in range(parts):
            start = pl.multiple_of(group_start(place_ref, k) + i * D, HEAD)
            out_ref[:, i * WIDE : (i + 1) * WIDE] = held_ref[:, pl.ds(start, WIDE)]


def modulated(active, weights):
    return [jnp.sum(weights * active[s], 0, keepdims=True) for s in range(STEPS)]


def open_kernel(
    place_ref, latent_ref, core_ref, chip_ref, taps_ref, q_gain_ref, k_gain_ref, w_mod_ref,
    w_qkv_ref, token_ref, mod_ref, gains_ref, mixed_ref, o0, o1, o2, o3,
    state_ref, conv_ref, q_held, k_held, normed_ref, held_ref, sems
):
    copies = [
        pltpu.make_async_copy(latent_ref, state_ref, sems.at[0]),
        pltpu.make_async_copy(taps_ref, conv_ref, sems.at[1]),
        pltpu.make_async_copy(q_gain_ref, q_held, sems.at[2]),
        pltpu.make_async_copy(k_gain_ref, k_held, sems.at[3]),
    ]
    for copy in copies:
        copy.start()
    active = [embedding(place_ref[2 + s]) for s in range(STEPS)]
    for i in range(4):
        here = slice(i * 2 * D // 4, (i + 1) * 2 * D // 4)
        for s, row in enumerate(modulated(active, w_mod_ref[:, here])):
            mod_ref[s : s + 1, here] = row
    for copy in copies:
        copy.wait()
    gains_ref[0:1, :] = (q_held[...] * (LOG2E / math.sqrt(HEAD))).reshape(1, D)
    gains_ref[1:2, :] = k_held[...].reshape(1, D)
    mix_rows(place_ref, state_ref, core_ref, chip_ref, conv_ref, mod_ref, mixed_ref, normed_ref, 0)
    for part in range(3):
        project(normed_ref[...], w_qkv_ref, gains_ref, part, held_ref, part * D)
    dealt(place_ref, held_ref, 3, (o0, o1, o2, o3))


def opening(where, state, core_rows, chip_rows, conv_weight, q_gain, k_gain, w_mod, w_qkv, token):
    return call(
        open_kernel,
        "opening",
        [SMEM, HBM, VMEM, VMEM] + [HBM] * 3 + [VMEM] * 2 + [ANY],
        [((STEPS, 2 * D), f32, VMEM), ((2, D), f32, VMEM), ((SLAB, D), f32, VMEM)]
        + [((SLAB, 3 * WIDE), bf16, VMEM)] * RING,
        [
            pltpu.VMEM((SLAB, D), bf16),
            pltpu.VMEM((3, D), f32),
            pltpu.VMEM((D,), f32),
            pltpu.VMEM((D,), f32),
            pltpu.VMEM((SLAB, D), bf16),
            pltpu.VMEM((SLAB, 3 * D), bf16),
            pltpu.SemaphoreType.DMA((4,)),
        ],
        us=10,
    )(
        where, in_hbm(state), core_rows, chip_rows, in_hbm(conv_weight), in_hbm(q_gain),
        in_hbm(k_gain), w_mod, w_qkv, token,
    )


def fill_bias(place_ref, counts_ref, bias_ref):
    z, c, y = place_ref[0], place_ref[1], place_ref[4]
    index = lax.broadcasted_iota(jnp.int32, (1, SLAB), 1)
    for a, (yy, cc) in enumerate(((y, c), (y, 1 - c), (1 - y, c), (1 - y, 1 - c))):
        for j in range(RING):
            slab = 8 * yy + 2 * ((z + RING - j) % RING) + cc
            here = slice(j * SLAB, (j + 1) * SLAB)
            row = jnp.where(index < counts_ref[slab], 0.0, masked_score)
            bias_ref[a : a + 1, here] = row
            if a == 0:
                for slot in range(RING):
                    bias_ref[4 + slot : 5 + slot, here] = (
                        jnp.full((1, SLAB), masked_score, f32) if slot == j else row
                    )
                if j == 0:
                    bias_ref[8:9, here] = row


def aside_kernel(place_ref, counts_ref, w_mod_ref, token_ref, gates_ref, bias_ref, held, sem):
    load = pltpu.make_async_copy(w_mod_ref.at[:, 2 * D :], held, sem)
    load.start()
    active = [embedding(place_ref[2 + s]) for s in range(STEPS)]
    fill_bias(place_ref, counts_ref, bias_ref)
    load.wait()
    for s, row in enumerate(modulated(active, held[...])):
        gates_ref[s : s + 1, :] = row


def aside(where, counts, w_mod, token):
    return call(
        aside_kernel,
        "aside",
        [SMEM, SMEM, HBM, ANY],
        [((STEPS, D), f32, VMEM), ((16, RING * SLAB), f32, VMEM)],
        [pltpu.VMEM((FREQ, D), f32), pltpu.SemaphoreType.DMA],
    )(where, counts, in_hbm(w_mod), token)


def next_kernel(
    place_ref, state_ref, core_ref, chip_ref, conv_ref, mod_ref, gains_ref, w_qkv_ref,
    mixed_ref, normed_ref, o0, o1, o2, o3, held_ref, *, row
):
    mix_rows(
        place_ref, state_ref, core_ref, chip_ref, conv_ref, mod_ref, mixed_ref, normed_ref, row
    )
    project(normed_ref[...], w_qkv_ref, gains_ref, 0, held_ref, 0)
    dealt(place_ref, held_ref, 1, (o0, o1, o2, o3))


def next_queries(where, state, core_rows, chip_rows, conv_weight, mod, gains, w_qkv, row):
    return call(
        functools.partial(next_kernel, row=row),
        "next_queries",
        [SMEM] + [VMEM] * 7,
        [((SLAB, D), f32, VMEM), ((SLAB, D), bf16, VMEM)] + [((SLAB, WIDE), bf16, VMEM)] * RING,
        [pltpu.VMEM((SLAB, D), bf16)],
    )(where, state, core_rows, chip_rows, conv_weight, mod, gains, w_qkv)


def dots(queries, keys):
    return lax.dot_general(queries, keys, (((1,), (1,)), ((), ())), preferred_element_type=f32)


def home_kernel(bias_ref, *refs):
    queries, keys, values = refs[:RING], refs[RING : 2 * RING], refs[2 * RING : 3 * RING]
    summed_ref, lse_ref = refs[-2:]
    bias = bias_ref[8:9, :SLAB]
    lanes = lax.broadcasted_iota(jnp.int32, (SLAB, HEAD), 1)
    ones = jnp.ones((SLAB, HEAD), bf16)
    heads = [slice(h * HEAD, (h + 1) * HEAD) for h in range(GROUP)]
    for pair in ((0, 1), (2, 3)):
        places = [(k, here) for k in pair for here in heads]
        first = keys[0].shape[1] - 2 * WIDE
        scores = [
            dots(queries[k][:, here], keys[k][:, first + here.start : first + here.stop]) + bias
            for k, here in places
        ]
        highest = [jnp.max(block, -1, keepdims=True) for block in scores]
        probs = [jnp.exp2(block - top).astype(bf16) for block, top in zip(scores, highest)]
        start = values[0].shape[1] - WIDE
        both = [
            jnp.dot(
                block,
                jnp.concatenate([values[k][:, start + here.start : start + here.stop], ones], 1),
                preferred_element_type=f32,
            )
            for block, (k, here) in zip(probs, places)
        ]
        for block, (k, here) in zip(both, places):
            summed_ref[:, k * WIDE + here.start : k * WIDE + here.stop] = (
                block[:, :HEAD] / block[:, HEAD:]
            )
        for i, k in enumerate(pair):
            lse = jnp.zeros((SLAB, HEAD), f32)
            for h in range(GROUP):
                n = i * GROUP + h
                lse = jnp.where(lanes == h, highest[n] + jnp.log2(both[n][:, HEAD:]), lse)
            lse_ref[:, k * HEAD : (k + 1) * HEAD] = lse


def at_home(bias, queries, keys, values, token):
    return call(
        home_kernel,
        "at_home",
        [VMEM] * (3 * RING + 1) + [ANY],
        [((SLAB, D), f32, VMEM), ((SLAB, RING * HEAD), f32, VMEM)],
    )(bias, *queries, *keys, *values, token)


def last_keys_kernel(
    place_ref, normed_ref, gains_ref, w_ref, token_ref, o0, o1, o2, o3, cache_ref, held_ref, sems
):
    writes = []
    for part in (1, 2):
        project(normed_ref[...], w_ref, gains_ref, part, held_ref, (part - 1) * D)
        columns = pl.ds((part - 1) * D, D)
        writes.append(
            pltpu.make_async_copy(
                held_ref.at[:, columns], cache_ref.at[:, columns], sems.at[part - 1]
            )
        )
        writes[-1].start()
    dealt(place_ref, held_ref, 2, (o0, o1, o2, o3))
    for write in writes:
        write.wait()


def last_keys(where, normed, gains, w_qkv, token):
    return call(
        last_keys_kernel,
        "last_keys",
        [SMEM] + [VMEM] * 3 + [ANY],
        [((SLAB, 2 * WIDE), bf16, VMEM)] * RING + [((SLAB, 2 * D), bf16, HBM)],
        [pltpu.VMEM((SLAB, 2 * D), bf16), pltpu.SemaphoreType.DMA((2,))],
    )(where, normed, gains, w_qkv, token)


def hold_kernel(*refs):
    pass


def held(array, tokens):
    return call(
        hold_kernel,
        "hold",
        [ANY] * (1 + len(tokens)),
        [(array.shape, array.dtype, ANY)],
        aliases={0: 0},
    )(array, *tokens)[0]


def stack_kernel(*refs):
    blocks, out_ref = refs[:RING], refs[-1]
    first = blocks[0].shape[1] - 2 * WIDE
    for k in range(RING):
        out_ref[k * SLAB : (k + 1) * SLAB, :] = blocks[k][:, first:]


def stack(blocks, token, us=0.1):
    return call(
        stack_kernel,
        "stack",
        [VMEM] * RING + [ANY],
        [((RING * SLAB, 2 * WIDE), bf16, VMEM)],
        us=us,
    )(*[blocks[k] for k in range(RING)], token)[0]


def attend_kernel(q0, q1, a0, a1, a2, a3, bias_ref, token_ref, *outs, slots):
    queries = (q0, q1)
    olds = (a0, a1, a2, a3)
    lanes = lax.broadcasted_iota(jnp.int32, (SLAB, HEAD), 1)
    ones = jnp.ones((RING * SLAB, HEAD), bf16)
    lse = [jnp.zeros((SLAB, HEAD), f32)] * 2
    for h in range(GROUP):
        here = slice(h * HEAD, (h + 1) * HEAD)
        there = slice(WIDE + h * HEAD, WIDE + (h + 1) * HEAD)
        keys = [old[:, here] for old in olds]
        values = [jnp.concatenate([old[:, there], ones], 1) for old in olds]
        joined = jnp.concatenate([query[:, here] for query in queries], 0)
        products = [dots(joined, keys[a]) for a in range(4)]
        for i, slot in enumerate(slots):
            scores = []
            for a in range(4):
                row = a if a else 4 + slot
                scores.append(products[a][i * SLAB : (i + 1) * SLAB] + bias_ref[row : row + 1, :])
            highest = functools.reduce(
                jnp.maximum, [jnp.max(block, -1, keepdims=True) for block in scores]
            )
            both = 0.0
            for a in range(4):
                probs = jnp.exp2(scores[a] - highest).astype(bf16)
                both += jnp.dot(probs, values[a], preferred_element_type=f32)
            total = both[:, HEAD:]
            outs[i][:, here] = (both[:, :HEAD] / total).astype(bf16)
            lse[i] = jnp.where(lanes == h, highest + jnp.log2(total), lse[i])
    for i in range(2):
        rest = lse[i]
        packed = 0.0
        for part in range(3):
            piece = rest.astype(bf16).astype(f32)
            rest = rest - piece
            packed += pltpu.roll(piece, part * GROUP, 1) if part else piece
        outs[i][:, WIDE:] = packed.astype(bf16)


def attend(queries, olds, bias, slots, token):
    return call(
        functools.partial(attend_kernel, slots=slots),
        "attend",
        [VMEM] * 7 + [ANY],
        [((SLAB, WIDE + HEAD), bf16, VMEM)] * 2,
        us=4,
    )(*[queries[k] for k in slots], *olds, bias, token)


def merged(away, summed_ref, lse_ref, k):
    pieces = away[:, WIDE:].astype(f32)
    lse = (
        pieces + pltpu.roll(pieces, HEAD - GROUP, 1) + pltpu.roll(pieces, HEAD - 2 * GROUP, 1)
    )
    share = 1.0 / (1.0 + jnp.exp2(lse_ref[:, k * HEAD : (k + 1) * HEAD] - lse))
    heads = []
    for h in range(GROUP):
        here = slice(k * WIDE + h * HEAD, k * WIDE + (h + 1) * HEAD)
        part = share[:, h : h + 1]
        heads.append(
            part * away[:, h * HEAD : (h + 1) * HEAD].astype(f32)
            + (1.0 - part) * summed_ref[:, here]
        )
    return jnp.concatenate(heads, 1).astype(bf16)


def early_output_kernel(place_ref, a0, a1, a2, w_ref, summed_ref, lse_ref, out_ref):
    total = 0.0
    for k, away in enumerate((a0, a1, a2)):
        weight = w_ref[pl.ds(group_start(place_ref, k), WIDE), :]
        total += jnp.dot(
            merged(away, summed_ref, lse_ref, k), weight, preferred_element_type=f32
        )
    out_ref[...] = total


def early_output(where, away, summed, lse, w_out):
    return call(
        early_output_kernel,
        "early_output",
        [SMEM] + [VMEM] * 6,
        [((SLAB, D), f32, VMEM)],
        us=3,
    )(where, away[0], away[1], away[2], w_out, summed, lse)[0]


def output_kernel(
    place_ref, away, w_ref, summed_ref, lse_ref, early_ref, mixed_ref, gates_ref, out_ref, *edges, row
):
    weight = w_ref[pl.ds(group_start(place_ref, 3), WIDE), :]
    total = early_ref[...] + jnp.dot(
        merged(away, summed_ref, lse_ref, 3), weight, preferred_element_type=f32
    )
    gate = gates_ref[row : row + 1, :]
    out_ref[...] = (mixed_ref[...] + gate * total).astype(bf16)
    if edges:
        for edge_ref, start in zip(edges, edge_starts(place_ref[1])):
            edge_ref[...] = out_ref[pl.ds(start, FRAME), :]


def output(where, away, summed, lse, w_out, early, mixed, gates, row):
    edge = ((FRAME, D), bf16, VMEM)
    return call(
        functools.partial(output_kernel, row=row),
        "output",
        [SMEM] + [VMEM] * 7,
        [((SLAB, D), bf16, VMEM)] + ([edge, edge] if row + 1 < STEPS else []),
    )(where, away[3], w_out, summed, lse, early, mixed, gates)


def sent(block, k):
    return lax.ppermute(block, "patch", ring(k % RING)) if k % RING else block


def shards(latent, stale_kv, timesteps, counts, conv_weight, w_mod, w_qkv, q_gain, k_gain, w_out):
    own_slab = lax.axis_index("patch")
    y, z, c = own_slab // 8, (own_slab // 2) % RING, own_slab % 2
    where = jnp.stack([z, c, timesteps[0], timesteps[1], y]).astype(jnp.int32)
    to_core, to_chip, *pieces = prepare(where, latent, stale_kv)
    chip_rows = lax.ppermute(to_chip, "patch", NEXT_CHIP)
    core_rows = lax.ppermute(to_core, "patch", CORE)
    arrived = {k: sent(pieces[k], k) for k in ORDER}
    old = stack(arrived, arrived[0], us=8)
    old_y = lax.ppermute(old, "patch", ACROSS)
    old_core = lax.ppermute(old, "patch", CORE)
    mod, gains, mixed, *blocks = opening(
        where, latent, core_rows, chip_rows, conv_weight, q_gain, k_gain, w_mod, w_qkv, old
    )
    fresh = {k: sent(blocks[k], k) for k in ORDER}
    gates, bias = aside(where, counts, w_mod, mixed)
    summed, lse = at_home(bias, blocks, blocks, blocks, mixed)
    new = stack(fresh, lse)
    new_y = lax.ppermute(new, "patch", ACROSS)
    new_core = lax.ppermute(new, "patch", CORE)
    old_y = held(old_y, [new])
    olds = [old, old_core, old_y, lax.ppermute(old_y, "patch", CORE)]
    far = attend(fresh, olds, bias, (2, 1), new)
    near = attend(fresh, olds, bias, (3, 0), far[0])
    away = {2: sent(far[0], -2), 1: sent(far[1], -1), 3: sent(near[0], -3), 0: near[1]}
    early = early_output(where, away, summed, lse, w_out)
    state, to_core, to_chip = output(where, away, summed, lse, w_out, early, mixed, gates, 0)

    chip_rows = lax.ppermute(to_chip, "patch", NEXT_CHIP)
    core_rows = lax.ppermute(to_core, "patch", CORE)
    mixed, normed, *own = next_queries(
        where, state, core_rows, chip_rows, conv_weight, mod, gains, w_qkv, 1
    )
    queries = {k: sent(own[k], k) for k in ORDER}
    new_y = held(new_y, own[:1])
    olds = [new, new_core, new_y, lax.ppermute(new_y, "patch", CORE)]
    *pairs, cache = last_keys(where, normed, gains, w_qkv, normed)
    far = attend(queries, olds, bias, (2, 1), pairs[1])
    near = attend(queries, olds, bias, (3, 0), far[0])
    away = {2: sent(far[0], -2), 1: sent(far[1], -1), 3: sent(near[0], -3), 0: near[1]}
    summed, lse = at_home(bias, own, pairs, pairs, normed)
    early = early_output(where, away, summed, lse, w_out)
    (state,) = output(where, away, summed, lse, w_out, early, mixed, gates, 1)
    return (state, cache)


def solution(mesh):
    rows = P(("req", "patch"), None)
    return jax.shard_map(
        shards,
        mesh=mesh,
        in_specs=(rows, rows, P("req"), P("req"), P(), P(), P(), P(), P(), P()),
        out_specs=(rows, rows),
        check_vma=False,
    )
```

```python
import functools
import math

import jax
import jax.numpy as jnp
from jax import lax
from jax.experimental import pallas as pl
from jax.experimental.pallas import tpu as pltpu
from jax.sharding import PartitionSpec as P

HEAD = 128
FREQ = 256
FRAME = 80
STEPS = 2
SLAB = 128
D = 1536
GROUP = 3
WIDE = GROUP * HEAD
RING = 4
LOG2E = math.log2(math.e)
ORDER = (2, 1, 3, 0)

epsilon = 1e-06
masked_score = -1e30
f32 = jnp.float32
bf16 = jnp.bfloat16


def place(y, z, c):
    return 8 * y + 2 * z + c


DEVICES = [(y, z, c) for y in range(2) for z in range(RING) for c in range(2)]
CORE = [(place(y, z, c), place(y, z, 1 - c)) for y, z, c in DEVICES]
ACROSS = [(place(y, z, c), place(1 - y, z, c)) for y, z, c in DEVICES]


def ring(k):
    return [(place(y, z, c), place(y, (z + k) % RING, c)) for y, z, c in DEVICES]


NEXT_CHIP = [(p, p + 1) for p in range(1, 15, 2)] + [(p + 1, p) for p in range(1, 15, 2)]


VMEM = pl.BlockSpec(memory_space=pltpu.VMEM)
SMEM = pl.BlockSpec(memory_space=pltpu.SMEM)
ANY = pl.BlockSpec(memory_space=pl.ANY)
HBM = pl.BlockSpec(memory_space=pltpu.HBM)


def cost(microseconds):
    return pl.CostEstimate(
        flops=int(microseconds * 1e9), bytes_accessed=int(microseconds * 1e6), transcendentals=0
    )


KEPT = "kept"


def in_vmem(array):
    return pltpu.with_memory_space_constraint(array, pltpu.VMEM)


def in_hbm(array):
    return pltpu.with_memory_space_constraint(array, pltpu.HBM)


def call(body, name, in_specs, outs, scratch=(), aliases=None, megabytes=10, us=0.1):
    return pl.pallas_call(
        body,
        in_specs=in_specs,
        out_specs=[VMEM if spec is KEPT else spec for _, _, spec in outs],
        out_shape=[
            (pltpu.VMEM if spec is KEPT else jax.ShapeDtypeStruct)(shape, dtype)
            for shape, dtype, spec in outs
        ],
        scratch_shapes=list(scratch),
        input_output_aliases=aliases or {},
        compiler_params=pltpu.CompilerParams(vmem_limit_bytes=megabytes * 2**20),
        cost_estimate=cost(us),
        name=name,
    )


def edge_starts(core):
    last = SLAB - FRAME
    return (
        pl.multiple_of(jnp.where(core == 0, last, 0), 16),
        pl.multiple_of(jnp.where(core == 0, 0, last), 16),
    )


def prepare_kernel(place_ref, latent_ref, stale_ref, core_ref, chip_ref, o0, o1, o2, o3, sems):
    outs = (o0, o1, o2, o3)
    core_start, chip_start = edge_starts(place_ref[1])
    copies = [
        pltpu.make_async_copy(latent_ref.at[pl.ds(chip_start, FRAME), :], chip_ref, sems.at[8]),
        pltpu.make_async_copy(latent_ref.at[pl.ds(core_start, FRAME), :], core_ref, sems.at[9]),
    ]
    for k in range(RING):
        start = (place_ref[0] + k) % RING * WIDE
        for part in range(2):
            columns = pl.ds(pl.multiple_of(start + part * D, HEAD), WIDE)
            copies.append(
                pltpu.make_async_copy(
                    stale_ref.at[:, columns],
                    outs[k].at[:, part * WIDE : (part + 1) * WIDE],
                    sems.at[2 * k + part],
                )
            )
    for copy in copies:
        copy.start()
    for copy in copies:
        copy.wait()


def prepare(where, latent, stale_kv):
    edge = ((FRAME, D), bf16, VMEM)
    return call(
        prepare_kernel,
        "prepare",
        [SMEM, HBM, HBM],
        [edge, edge] + [((SLAB, 2 * WIDE), bf16, VMEM)] * RING,
        [pltpu.SemaphoreType.DMA((10,))],
        us=8,
    )(where, in_hbm(latent), in_hbm(stale_kv))


def mix_rows(place_ref, state_ref, core_ref, chip_ref, conv_ref, mod_ref, mixed_ref, normed_ref, row):
    first = place_ref[1] == 0
    state = state_ref[...].astype(f32)
    core_rows = core_ref[...].astype(f32)
    chip_rows = chip_ref[...].astype(f32)
    above = jnp.where(first, chip_rows, core_rows)
    below = jnp.where(first, core_rows, chip_rows)
    before = jnp.concatenate([above, state[: SLAB - FRAME]], 0)
    after_rows = jnp.concatenate([state[FRAME:], below], 0)
    mixed = (
        state
        + conv_ref[0:1, :] * before
        + conv_ref[1:2, :] * state
        + conv_ref[2:3, :] * after_rows
    )
    mixed_ref[...] = mixed
    shift = mod_ref[row : row + 1, :D]
    scale = mod_ref[row : row + 1, D : 2 * D]
    centred = mixed - jnp.mean(mixed, -1, keepdims=True)
    variance = jnp.mean(centred * centred, -1, keepdims=True)
    normed_ref[...] = (centred * lax.rsqrt(variance + epsilon) * (1.0 + scale) + shift).astype(bf16)


def embedding(moment):
    halfway = FREQ // 2
    index = lax.broadcasted_iota(jnp.int32, (halfway, 1), 0).astype(f32)
    angles = moment.astype(f32) * jnp.exp(-math.log(10000.0) * index / halfway)
    values = jnp.concatenate([jnp.cos(angles), jnp.sin(angles)], 0)
    return values / (1.0 + jnp.exp(-values))


def head_normed(block, gain):
    mean_square = jnp.mean(block * block, -1, keepdims=True)
    return (block * lax.rsqrt(mean_square + epsilon) * gain).astype(bf16)


def normed_heads(normed, weight, gain_ref, row, group, out_ref, start):
    block = jnp.dot(normed, weight, preferred_element_type=f32)
    gain = gain_ref[row : row + 1, pl.ds(group, WIDE)]
    for h in range(GROUP):
        here = slice(h * HEAD, (h + 1) * HEAD)
        out_ref[:, start + h * HEAD : start + (h + 1) * HEAD] = head_normed(
            block[:, here], gain[:, here]
        )


def group_start(place_ref, k):
    return pl.multiple_of((place_ref[0] + k) % RING * WIDE, HEAD)


def project(normed, w_ref, gains_ref, part, held_ref, first):
    block = jnp.dot(normed, w_ref[:, part * D : (part + 1) * D], preferred_element_type=f32)
    if part == 2:
        held_ref[:, first : first + D] = block.astype(bf16)
        return
    for h in range(D // HEAD):
        here = slice(h * HEAD, (h + 1) * HEAD)
        held_ref[:, first + here.start : first + here.stop] = head_normed(
            block[:, here], gains_ref[part : part + 1, here]
        )


def dealt(place_ref, held_ref, parts, outs):
    for k, out_ref in enumerate(outs):
        for i in range(parts):
            start = pl.multiple_of(group_start(place_ref, k) + i * D, HEAD)
            out_ref[:, i * WIDE : (i + 1) * WIDE] = held_ref[:, pl.ds(start, WIDE)]


def modulated(active, weights):
    return [jnp.sum(weights * active[s], 0, keepdims=True) for s in range(STEPS)]


def open_kernel(
    place_ref, latent_ref, core_ref, chip_ref, taps_ref, q_gain_ref, k_gain_ref, w_mod_ref,
    w_qkv_ref, token_ref, mod_ref, gains_ref, mixed_ref, o0, o1, o2, o3,
    state_ref, conv_ref, q_held, k_held, normed_ref, held_ref, sems
):
    copies = [
        pltpu.make_async_copy(latent_ref, state_ref, sems.at[0]),
        pltpu.make_async_copy(taps_ref, conv_ref, sems.at[1]),
        pltpu.make_async_copy(q_gain_ref, q_held, sems.at[2]),
        pltpu.make_async_copy(k_gain_ref, k_held, sems.at[3]),
    ]
    for copy in copies:
        copy.start()
    active = [embedding(place_ref[2 + s]) for s in range(STEPS)]
    for i in range(4):
        here = slice(i * 2 * D // 4, (i + 1) * 2 * D // 4)
        for s, row in enumerate(modulated(active, w_mod_ref[:, here])):
            mod_ref[s : s + 1, here] = row
    for copy in copies:
        copy.wait()
    gains_ref[0:1, :] = (q_held[...] * (LOG2E / math.sqrt(HEAD))).reshape(1, D)
    gains_ref[1:2, :] = k_held[...].reshape(1, D)
    mix_rows(place_ref, state_ref, core_ref, chip_ref, conv_ref, mod_ref, mixed_ref, normed_ref, 0)
    for part in range(3):
        project(normed_ref[...], w_qkv_ref, gains_ref, part, held_ref, part * D)
    dealt(place_ref, held_ref, 3, (o0, o1, o2, o3))


def opening(where, state, core_rows, chip_rows, conv_weight, q_gain, k_gain, w_mod, w_qkv, token):
    return call(
        open_kernel,
        "opening",
        [SMEM, HBM, VMEM, VMEM] + [HBM] * 3 + [VMEM] * 2 + [ANY],
        [((STEPS, 2 * D), f32, VMEM), ((2, D), f32, VMEM), ((SLAB, D), f32, VMEM)]
        + [((SLAB, 3 * WIDE), bf16, VMEM)] * RING,
        [
            pltpu.VMEM((SLAB, D), bf16),
            pltpu.VMEM((3, D), f32),
            pltpu.VMEM((D,), f32),
            pltpu.VMEM((D,), f32),
            pltpu.VMEM((SLAB, D), bf16),
            pltpu.VMEM((SLAB, 3 * D), bf16),
            pltpu.SemaphoreType.DMA((4,)),
        ],
        us=10,
    )(
        where, in_hbm(state), core_rows, chip_rows, in_hbm(conv_weight), in_hbm(q_gain),
        in_hbm(k_gain), w_mod, w_qkv, token,
    )


def fill_bias(place_ref, counts_ref, bias_ref):
    z, c, y = place_ref[0], place_ref[1], place_ref[4]
    index = lax.broadcasted_iota(jnp.int32, (1, SLAB), 1)
    for a, (yy, cc) in enumerate(((y, c), (y, 1 - c), (1 - y, c), (1 - y, 1 - c))):
        for j in range(RING):
            slab = 8 * yy + 2 * ((z + RING - j) % RING) + cc
            here = slice(j * SLAB, (j + 1) * SLAB)
            row = jnp.where(index < counts_ref[slab], 0.0, masked_score)
            bias_ref[a : a + 1, here] = row
            if a == 0:
                for slot in range(RING):
                    bias_ref[4 + slot : 5 + slot, here] = (
                        jnp.full((1, SLAB), masked_score, f32) if slot == j else row
                    )
                if j == 0:
                    bias_ref[8:9, here] = row


def aside_kernel(place_ref, counts_ref, w_mod_ref, token_ref, gates_ref, bias_ref, held, sem):
    load = pltpu.make_async_copy(w_mod_ref.at[:, 2 * D :], held, sem)
    load.start()
    active = [embedding(place_ref[2 + s]) for s in range(STEPS)]
    fill_bias(place_ref, counts_ref, bias_ref)
    load.wait()
    for s, row in enumerate(modulated(active, held[...])):
        gates_ref[s : s + 1, :] = row


def aside(where, counts, w_mod, token):
    return call(
        aside_kernel,
        "aside",
        [SMEM, SMEM, HBM, ANY],
        [((STEPS, D), f32, VMEM), ((16, RING * SLAB), f32, VMEM)],
        [pltpu.VMEM((FREQ, D), f32), pltpu.SemaphoreType.DMA],
    )(where, counts, in_hbm(w_mod), token)


def next_kernel(
    place_ref, state_ref, core_ref, chip_ref, conv_ref, mod_ref, gains_ref, w_qkv_ref,
    mixed_ref, normed_ref, o0, o1, o2, o3, held_ref, *, row
):
    mix_rows(
        place_ref, state_ref, core_ref, chip_ref, conv_ref, mod_ref, mixed_ref, normed_ref, row
    )
    project(normed_ref[...], w_qkv_ref, gains_ref, 0, held_ref, 0)
    dealt(place_ref, held_ref, 1, (o0, o1, o2, o3))


def next_queries(where, state, core_rows, chip_rows, conv_weight, mod, gains, w_qkv, row):
    return call(
        functools.partial(next_kernel, row=row),
        "next_queries",
        [SMEM] + [VMEM] * 7,
        [((SLAB, D), f32, VMEM), ((SLAB, D), bf16, VMEM)] + [((SLAB, WIDE), bf16, VMEM)] * RING,
        [pltpu.VMEM((SLAB, D), bf16)],
    )(where, state, core_rows, chip_rows, conv_weight, mod, gains, w_qkv)


def dots(queries, keys):
    return lax.dot_general(queries, keys, (((1,), (1,)), ((), ())), preferred_element_type=f32)


def home_kernel(bias_ref, *refs):
    queries, keys, values = refs[:RING], refs[RING : 2 * RING], refs[2 * RING : 3 * RING]
    summed_ref, lse_ref = refs[-2:]
    bias = bias_ref[8:9, :SLAB]
    lanes = lax.broadcasted_iota(jnp.int32, (SLAB, HEAD), 1)
    ones = jnp.ones((SLAB, HEAD), bf16)
    heads = [slice(h * HEAD, (h + 1) * HEAD) for h in range(GROUP)]
    for pair in ((0, 1), (2, 3)):
        places = [(k, here) for k in pair for here in heads]
        first = keys[0].shape[1] - 2 * WIDE
        scores = [
            dots(queries[k][:, here], keys[k][:, first + here.start : first + here.stop]) + bias
            for k, here in places
        ]
        highest = [jnp.max(block, -1, keepdims=True) for block in scores]
        probs = [jnp.exp2(block - top).astype(bf16) for block, top in zip(scores, highest)]
        start = values[0].shape[1] - WIDE
        both = [
            jnp.dot(
                block,
                jnp.concatenate([values[k][:, start + here.start : start + here.stop], ones], 1),
                preferred_element_type=f32,
            )
            for block, (k, here) in zip(probs, places)
        ]
        for block, (k, here) in zip(both, places):
            summed_ref[:, k * WIDE + here.start : k * WIDE + here.stop] = (
                block[:, :HEAD] / block[:, HEAD:]
            )
        for i, k in enumerate(pair):
            lse = jnp.zeros((SLAB, HEAD), f32)
            for h in range(GROUP):
                n = i * GROUP + h
                lse = jnp.where(lanes == h, highest[n] + jnp.log2(both[n][:, HEAD:]), lse)
            lse_ref[:, k * HEAD : (k + 1) * HEAD] = lse


def at_home(bias, queries, keys, values, token):
    return call(
        home_kernel,
        "at_home",
        [VMEM] * (3 * RING + 1) + [ANY],
        [((SLAB, D), f32, VMEM), ((SLAB, RING * HEAD), f32, VMEM)],
    )(bias, *queries, *keys, *values, token)


def last_keys_kernel(
    place_ref, normed_ref, gains_ref, w_ref, token_ref, o0, o1, o2, o3, cache_ref, held_ref, sems
):
    writes = []
    for part in (1, 2):
        project(normed_ref[...], w_ref, gains_ref, part, held_ref, (part - 1) * D)
        columns = pl.ds((part - 1) * D, D)
        writes.append(
            pltpu.make_async_copy(
                held_ref.at[:, columns], cache_ref.at[:, columns], sems.at[part - 1]
            )
        )
        writes[-1].start()
    dealt(place_ref, held_ref, 2, (o0, o1, o2, o3))
    for write in writes:
        write.wait()


def last_keys(where, normed, gains, w_qkv, token):
    return call(
        last_keys_kernel,
        "last_keys",
        [SMEM] + [VMEM] * 3 + [ANY],
        [((SLAB, 2 * WIDE), bf16, VMEM)] * RING + [((SLAB, 2 * D), bf16, HBM)],
        [pltpu.VMEM((SLAB, 2 * D), bf16), pltpu.SemaphoreType.DMA((2,))],
    )(where, normed, gains, w_qkv, token)


def hold_kernel(*refs):
    pass


def held(array, tokens):
    return call(
        hold_kernel,
        "hold",
        [ANY] * (1 + len(tokens)),
        [(array.shape, array.dtype, ANY)],
        aliases={0: 0},
    )(array, *tokens)[0]


def stack_kernel(*refs):
    blocks, out_ref = refs[:RING], refs[-1]
    first = blocks[0].shape[1] - 2 * WIDE
    for k, block in zip(ORDER, blocks):
        out_ref[k * SLAB : (k + 1) * SLAB, :] = block[:, first:]


def stack(blocks, token, us=0.1):
    return call(
        stack_kernel,
        "stack",
        [VMEM] * RING + [ANY],
        [((RING * SLAB, 2 * WIDE), bf16, VMEM)],
        us=us,
    )(*[blocks[k] for k in ORDER], token)[0]


def attend_kernel(token_ref, q0, q1, a0, a1, a2, a3, bias_ref, *outs, slots):
    queries = (q0, q1)
    olds = (a0, a1, a2, a3)
    lanes = lax.broadcasted_iota(jnp.int32, (SLAB, HEAD), 1)
    ones = jnp.ones((RING * SLAB, HEAD), bf16)
    lse = [jnp.zeros((SLAB, HEAD), f32)] * 2
    for h in range(GROUP):
        here = slice(h * HEAD, (h + 1) * HEAD)
        there = slice(WIDE + h * HEAD, WIDE + (h + 1) * HEAD)
        keys = [old[:, here] for old in olds]
        values = [jnp.concatenate([old[:, there], ones], 1) for old in olds]
        joined = jnp.concatenate([query[:, here] for query in queries], 0)
        products = [dots(joined, keys[a]) for a in range(4)]
        for i, slot in enumerate(slots):
            scores = []
            for a in range(4):
                row = a if a else 4 + slot
                scores.append(products[a][i * SLAB : (i + 1) * SLAB] + bias_ref[row : row + 1, :])
            highest = functools.reduce(
                jnp.maximum, [jnp.max(block, -1, keepdims=True) for block in scores]
            )
            both = 0.0
            for a in range(4):
                probs = jnp.exp2(scores[a] - highest).astype(bf16)
                both += jnp.dot(probs, values[a], preferred_element_type=f32)
            total = both[:, HEAD:]
            outs[i][:, here] = (both[:, :HEAD] / total).astype(bf16)
            lse[i] = jnp.where(lanes == h, highest + jnp.log2(total), lse[i])
    for i in range(2):
        rest = lse[i]
        packed = 0.0
        for part in range(3):
            piece = rest.astype(bf16).astype(f32)
            rest = rest - piece
            packed += pltpu.roll(piece, part * GROUP, 1) if part else piece
        outs[i][:, WIDE:] = packed.astype(bf16)


def attend(queries, olds, bias, slots, token):
    return call(
        functools.partial(attend_kernel, slots=slots),
        "attend",
        [ANY] + [VMEM] * 7,
        [((SLAB, WIDE + HEAD), bf16, VMEM)] * 2,
        us=4,
    )(token, *[queries[k] for k in slots], *olds, bias)


def merged(away, summed_ref, lse_ref, k):
    pieces = away[:, WIDE:].astype(f32)
    lse = (
        pieces + pltpu.roll(pieces, HEAD - GROUP, 1) + pltpu.roll(pieces, HEAD - 2 * GROUP, 1)
    )
    share = 1.0 / (1.0 + jnp.exp2(lse_ref[:, k * HEAD : (k + 1) * HEAD] - lse))
    heads = []
    for h in range(GROUP):
        here = slice(k * WIDE + h * HEAD, k * WIDE + (h + 1) * HEAD)
        part = share[:, h : h + 1]
        heads.append(
            part * away[:, h * HEAD : (h + 1) * HEAD].astype(f32)
            + (1.0 - part) * summed_ref[:, here]
        )
    return jnp.concatenate(heads, 1).astype(bf16)


def early_output_kernel(place_ref, a2, a1, a0, w_ref, summed_ref, lse_ref, out_ref):
    total = 0.0
    for k, away in enumerate((a0, a1, a2)):
        weight = w_ref[pl.ds(group_start(place_ref, k), WIDE), :]
        total += jnp.dot(
            merged(away, summed_ref, lse_ref, k), weight, preferred_element_type=f32
        )
    out_ref[...] = total


def early_output(where, away, summed, lse, w_out):
    return call(
        early_output_kernel,
        "early_output",
        [SMEM] + [VMEM] * 6,
        [((SLAB, D), f32, VMEM)],
        us=3,
    )(where, away[2], away[1], away[0], w_out, summed, lse)[0]


def output_kernel(
    place_ref, away, w_ref, summed_ref, lse_ref, early_ref, mixed_ref, gates_ref, out_ref, *edges, row
):
    weight = w_ref[pl.ds(group_start(place_ref, 3), WIDE), :]
    total = early_ref[...] + jnp.dot(
        merged(away, summed_ref, lse_ref, 3), weight, preferred_element_type=f32
    )
    gate = gates_ref[row : row + 1, :]
    out_ref[...] = (mixed_ref[...] + gate * total).astype(bf16)
    if edges:
        for edge_ref, start in zip(edges, edge_starts(place_ref[1])):
            edge_ref[...] = out_ref[pl.ds(start, FRAME), :]


def output(where, away, summed, lse, w_out, early, mixed, gates, row):
    edge = ((FRAME, D), bf16, VMEM)
    return call(
        functools.partial(output_kernel, row=row),
        "output",
        [SMEM] + [VMEM] * 7,
        [((SLAB, D), bf16, VMEM)] + ([edge, edge] if row + 1 < STEPS else []),
    )(where, away[3], w_out, summed, lse, early, mixed, gates)


def sent(block, k):
    return lax.ppermute(block, "patch", ring(k % RING)) if k % RING else block


def shards(latent, stale_kv, timesteps, counts, conv_weight, w_mod, w_qkv, q_gain, k_gain, w_out):
    own_slab = lax.axis_index("patch")
    y, z, c = own_slab // 8, (own_slab // 2) % RING, own_slab % 2
    where = jnp.stack([z, c, timesteps[0], timesteps[1], y]).astype(jnp.int32)
    to_core, to_chip, *pieces = prepare(where, latent, stale_kv)
    chip_rows = lax.ppermute(to_chip, "patch", NEXT_CHIP)
    core_rows = lax.ppermute(to_core, "patch", CORE)
    arrived = {k: sent(pieces[k], k) for k in ORDER}
    old = stack(arrived, arrived[0], us=8)
    old_y = lax.ppermute(old, "patch", ACROSS)
    old_core = lax.ppermute(old, "patch", CORE)
    mod, gains, mixed, *blocks = opening(
        where, latent, core_rows, chip_rows, conv_weight, q_gain, k_gain, w_mod, w_qkv, old
    )
    fresh = {k: sent(blocks[k], k) for k in ORDER}
    gates, bias = aside(where, counts, w_mod, mixed)
    summed, lse = at_home(bias, blocks, blocks, blocks, mixed)
    new = stack(fresh, lse)
    new_y = lax.ppermute(new, "patch", ACROSS)
    new_core = lax.ppermute(new, "patch", CORE)
    old_y = held(old_y, [new])
    olds = [old, old_core, old_y, lax.ppermute(old_y, "patch", CORE)]
    far = attend(fresh, olds, bias, (2, 1), new)
    near = attend(fresh, olds, bias, (3, 0), far[0])
    away = {2: sent(far[0], -2), 1: sent(far[1], -1), 3: sent(near[0], -3), 0: near[1]}
    early = early_output(where, away, summed, lse, w_out)
    state, to_core, to_chip = output(where, away, summed, lse, w_out, early, mixed, gates, 0)

    chip_rows = lax.ppermute(to_chip, "patch", NEXT_CHIP)
    core_rows = lax.ppermute(to_core, "patch", CORE)
    mixed, normed, *own = next_queries(
        where, state, core_rows, chip_rows, conv_weight, mod, gains, w_qkv, 1
    )
    queries = {k: sent(own[k], k) for k in ORDER}
    new_y = held(new_y, own[:1])
    olds = [new, new_core, new_y, lax.ppermute(new_y, "patch", CORE)]
    *pairs, cache = last_keys(where, normed, gains, w_qkv, normed)
    far = attend(queries, olds, bias, (2, 1), pairs[1])
    near = attend(queries, olds, bias, (3, 0), far[0])
    away = {2: sent(far[0], -2), 1: sent(far[1], -1), 3: sent(near[0], -3), 0: near[1]}
    summed, lse = at_home(bias, own, pairs, pairs, normed)
    early = early_output(where, away, summed, lse, w_out)
    (state,) = output(where, away, summed, lse, w_out, early, mixed, gates, 1)
    return (state, cache)


def solution(mesh):
    rows = P(("req", "patch"), None)
    return jax.shard_map(
        shards,
        mesh=mesh,
        in_specs=(rows, rows, P("req"), P("req"), P(), P(), P(), P(), P(), P()),
        out_specs=(rows, rows),
        check_vma=False,
    )
```

```python
import functools
import math

import jax
import jax.numpy as jnp
from jax import lax
from jax.experimental import pallas as pl
from jax.experimental.pallas import tpu as pltpu
from jax.sharding import PartitionSpec as P

HEAD = 128
FREQ = 256
FRAME = 80
STEPS = 2
SLAB = 128
D = 1536
GROUP = 3
WIDE = GROUP * HEAD
RING = 4
LOG2E = math.log2(math.e)
ORDER = (2, 1, 3, 0)

epsilon = 1e-06
masked_score = -1e30
f32 = jnp.float32
bf16 = jnp.bfloat16


def place(y, z, c):
    return 8 * y + 2 * z + c


DEVICES = [(y, z, c) for y in range(2) for z in range(RING) for c in range(2)]
CORE = [(place(y, z, c), place(y, z, 1 - c)) for y, z, c in DEVICES]
ACROSS = [(place(y, z, c), place(1 - y, z, c)) for y, z, c in DEVICES]


def ring(k):
    return [(place(y, z, c), place(y, (z + k) % RING, c)) for y, z, c in DEVICES]


NEXT_CHIP = [(p, p + 1) for p in range(1, 15, 2)] + [(p + 1, p) for p in range(1, 15, 2)]


VMEM = pl.BlockSpec(memory_space=pltpu.VMEM)
SMEM = pl.BlockSpec(memory_space=pltpu.SMEM)
ANY = pl.BlockSpec(memory_space=pl.ANY)
HBM = pl.BlockSpec(memory_space=pltpu.HBM)


def cost(microseconds):
    return pl.CostEstimate(
        flops=int(microseconds * 1e9), bytes_accessed=int(microseconds * 1e6), transcendentals=0
    )


KEPT = "kept"


def in_vmem(array):
    return pltpu.with_memory_space_constraint(array, pltpu.VMEM)


def in_hbm(array):
    return pltpu.with_memory_space_constraint(array, pltpu.HBM)


def call(body, name, in_specs, outs, scratch=(), aliases=None, megabytes=10, us=0.1):
    return pl.pallas_call(
        body,
        in_specs=in_specs,
        out_specs=[VMEM if spec is KEPT else spec for _, _, spec in outs],
        out_shape=[
            (pltpu.VMEM if spec is KEPT else jax.ShapeDtypeStruct)(shape, dtype)
            for shape, dtype, spec in outs
        ],
        scratch_shapes=list(scratch),
        input_output_aliases=aliases or {},
        compiler_params=pltpu.CompilerParams(vmem_limit_bytes=megabytes * 2**20),
        cost_estimate=cost(us),
        name=name,
    )


def edge_starts(core):
    last = SLAB - FRAME
    return (
        pl.multiple_of(jnp.where(core == 0, last, 0), 16),
        pl.multiple_of(jnp.where(core == 0, 0, last), 16),
    )


def prepare_kernel(place_ref, latent_ref, stale_ref, core_ref, chip_ref, o0, o1, o2, o3, sems):
    outs = (o0, o1, o2, o3)
    core_start, chip_start = edge_starts(place_ref[1])
    copies = [
        pltpu.make_async_copy(latent_ref.at[pl.ds(chip_start, FRAME), :], chip_ref, sems.at[8]),
        pltpu.make_async_copy(latent_ref.at[pl.ds(core_start, FRAME), :], core_ref, sems.at[9]),
    ]
    for k in range(RING):
        start = (place_ref[0] + k) % RING * WIDE
        for part in range(2):
            columns = pl.ds(pl.multiple_of(start + part * D, HEAD), WIDE)
            copies.append(
                pltpu.make_async_copy(
                    stale_ref.at[:, columns],
                    outs[k].at[:, part * WIDE : (part + 1) * WIDE],
                    sems.at[2 * k + part],
                )
            )
    for copy in copies:
        copy.start()
    for copy in copies:
        copy.wait()


def prepare(where, latent, stale_kv):
    edge = ((FRAME, D), bf16, VMEM)
    return call(
        prepare_kernel,
        "prepare",
        [SMEM, HBM, HBM],
        [edge, edge] + [((SLAB, 2 * WIDE), bf16, VMEM)] * RING,
        [pltpu.SemaphoreType.DMA((10,))],
        us=8,
    )(where, in_hbm(latent), in_hbm(stale_kv))


def mix_rows(place_ref, state_ref, core_ref, chip_ref, conv_ref, mod_ref, mixed_ref, normed_ref, row):
    first = place_ref[1] == 0
    state = state_ref[...].astype(f32)
    core_rows = core_ref[...].astype(f32)
    chip_rows = chip_ref[...].astype(f32)
    above = jnp.where(first, chip_rows, core_rows)
    below = jnp.where(first, core_rows, chip_rows)
    before = jnp.concatenate([above, state[: SLAB - FRAME]], 0)
    after_rows = jnp.concatenate([state[FRAME:], below], 0)
    mixed = (
        state
        + conv_ref[0:1, :] * before
        + conv_ref[1:2, :] * state
        + conv_ref[2:3, :] * after_rows
    )
    mixed_ref[...] = mixed
    shift = mod_ref[row : row + 1, :D]
    scale = mod_ref[row : row + 1, D : 2 * D]
    centred = mixed - jnp.mean(mixed, -1, keepdims=True)
    variance = jnp.mean(centred * centred, -1, keepdims=True)
    normed_ref[...] = (centred * lax.rsqrt(variance + epsilon) * (1.0 + scale) + shift).astype(bf16)


def embedding(moment):
    halfway = FREQ // 2
    index = lax.broadcasted_iota(jnp.int32, (halfway, 1), 0).astype(f32)
    angles = moment.astype(f32) * jnp.exp(-math.log(10000.0) * index / halfway)
    values = jnp.concatenate([jnp.cos(angles), jnp.sin(angles)], 0)
    return values / (1.0 + jnp.exp(-values))


def head_normed(block, gain):
    mean_square = jnp.mean(block * block, -1, keepdims=True)
    return (block * lax.rsqrt(mean_square + epsilon) * gain).astype(bf16)


def normed_heads(normed, weight, gain_ref, row, group, out_ref, start):
    block = jnp.dot(normed, weight, preferred_element_type=f32)
    gain = gain_ref[row : row + 1, pl.ds(group, WIDE)]
    for h in range(GROUP):
        here = slice(h * HEAD, (h + 1) * HEAD)
        out_ref[:, start + h * HEAD : start + (h + 1) * HEAD] = head_normed(
            block[:, here], gain[:, here]
        )


def group_start(place_ref, k):
    return pl.multiple_of((place_ref[0] + k) % RING * WIDE, HEAD)


def project(normed, w_ref, gains_ref, part, held_ref, first):
    block = jnp.dot(normed, w_ref[:, part * D : (part + 1) * D], preferred_element_type=f32)
    if part == 2:
        held_ref[:, first : first + D] = block.astype(bf16)
        return
    for h in range(D // HEAD):
        here = slice(h * HEAD, (h + 1) * HEAD)
        held_ref[:, first + here.start : first + here.stop] = head_normed(
            block[:, here], gains_ref[part : part + 1, here]
        )


def dealt(place_ref, held_ref, parts, outs):
    for k, out_ref in enumerate(outs):
        for i in range(parts):
            start = pl.multiple_of(group_start(place_ref, k) + i * D, HEAD)
            out_ref[:, i * WIDE : (i + 1) * WIDE] = held_ref[:, pl.ds(start, WIDE)]


def modulated(active, weights):
    return [jnp.sum(weights * active[s], 0, keepdims=True) for s in range(STEPS)]


def open_kernel(
    place_ref, latent_ref, core_ref, chip_ref, taps_ref, q_gain_ref, k_gain_ref, w_mod_ref,
    w_qkv_ref, token_ref, mod_ref, gains_ref, mixed_ref, o0, o1, o2, o3,
    state_ref, conv_ref, q_held, k_held, normed_ref, held_ref, sems
):
    copies = [
        pltpu.make_async_copy(latent_ref, state_ref, sems.at[0]),
        pltpu.make_async_copy(taps_ref, conv_ref, sems.at[1]),
        pltpu.make_async_copy(q_gain_ref, q_held, sems.at[2]),
        pltpu.make_async_copy(k_gain_ref, k_held, sems.at[3]),
    ]
    for copy in copies:
        copy.start()
    active = [embedding(place_ref[2 + s]) for s in range(STEPS)]
    for i in range(4):
        here = slice(i * 2 * D // 4, (i + 1) * 2 * D // 4)
        for s, row in enumerate(modulated(active, w_mod_ref[:, here])):
            mod_ref[s : s + 1, here] = row
    for copy in copies:
        copy.wait()
    gains_ref[0:1, :] = (q_held[...] * (LOG2E / math.sqrt(HEAD))).reshape(1, D)
    gains_ref[1:2, :] = k_held[...].reshape(1, D)
    mix_rows(place_ref, state_ref, core_ref, chip_ref, conv_ref, mod_ref, mixed_ref, normed_ref, 0)
    for part in range(3):
        project(normed_ref[...], w_qkv_ref, gains_ref, part, held_ref, part * D)
    dealt(place_ref, held_ref, 3, (o0, o1, o2, o3))


def opening(where, state, core_rows, chip_rows, conv_weight, q_gain, k_gain, w_mod, w_qkv, token):
    return call(
        open_kernel,
        "opening",
        [SMEM, HBM, VMEM, VMEM] + [HBM] * 3 + [VMEM] * 2 + [ANY],
        [((STEPS, 2 * D), f32, VMEM), ((2, D), f32, VMEM), ((SLAB, D), f32, VMEM)]
        + [((SLAB, 3 * WIDE), bf16, VMEM)] * RING,
        [
            pltpu.VMEM((SLAB, D), bf16),
            pltpu.VMEM((3, D), f32),
            pltpu.VMEM((D,), f32),
            pltpu.VMEM((D,), f32),
            pltpu.VMEM((SLAB, D), bf16),
            pltpu.VMEM((SLAB, 3 * D), bf16),
            pltpu.SemaphoreType.DMA((4,)),
        ],
        us=10,
    )(
        where, in_hbm(state), core_rows, chip_rows, in_hbm(conv_weight), in_hbm(q_gain),
        in_hbm(k_gain), w_mod, w_qkv, token,
    )


def fill_bias(place_ref, counts_ref, bias_ref):
    z, c, y = place_ref[0], place_ref[1], place_ref[4]
    index = lax.broadcasted_iota(jnp.int32, (1, SLAB), 1)
    for a, (yy, cc) in enumerate(((y, c), (y, 1 - c), (1 - y, c), (1 - y, 1 - c))):
        for j in range(RING):
            slab = 8 * yy + 2 * ((z + RING - j) % RING) + cc
            here = slice(j * SLAB, (j + 1) * SLAB)
            row = jnp.where(index < counts_ref[slab], 0.0, masked_score)
            bias_ref[a : a + 1, here] = row
            if a == 0:
                for slot in range(RING):
                    bias_ref[4 + slot : 5 + slot, here] = (
                        jnp.full((1, SLAB), masked_score, f32) if slot == j else row
                    )
                if j == 0:
                    bias_ref[8:9, here] = row


def aside_kernel(place_ref, counts_ref, w_mod_ref, token_ref, gates_ref, bias_ref, held, sem):
    load = pltpu.make_async_copy(w_mod_ref.at[:, 2 * D :], held, sem)
    load.start()
    active = [embedding(place_ref[2 + s]) for s in range(STEPS)]
    fill_bias(place_ref, counts_ref, bias_ref)
    load.wait()
    for s, row in enumerate(modulated(active, held[...])):
        gates_ref[s : s + 1, :] = row


def aside(where, counts, w_mod, token):
    return call(
        aside_kernel,
        "aside",
        [SMEM, SMEM, HBM, ANY],
        [((STEPS, D), f32, VMEM), ((16, RING * SLAB), f32, VMEM)],
        [pltpu.VMEM((FREQ, D), f32), pltpu.SemaphoreType.DMA],
    )(where, counts, in_hbm(w_mod), token)


def next_kernel(
    place_ref, state_ref, core_ref, chip_ref, conv_ref, mod_ref, gains_ref, w_qkv_ref,
    mixed_ref, normed_ref, o0, o1, o2, o3, held_ref, *, row
):
    mix_rows(
        place_ref, state_ref, core_ref, chip_ref, conv_ref, mod_ref, mixed_ref, normed_ref, row
    )
    project(normed_ref[...], w_qkv_ref, gains_ref, 0, held_ref, 0)
    dealt(place_ref, held_ref, 1, (o0, o1, o2, o3))


def next_queries(where, state, core_rows, chip_rows, conv_weight, mod, gains, w_qkv, row):
    return call(
        functools.partial(next_kernel, row=row),
        "next_queries",
        [SMEM] + [VMEM] * 7,
        [((SLAB, D), f32, VMEM), ((SLAB, D), bf16, VMEM)] + [((SLAB, WIDE), bf16, VMEM)] * RING,
        [pltpu.VMEM((SLAB, D), bf16)],
    )(where, state, core_rows, chip_rows, conv_weight, mod, gains, w_qkv)


def dots(queries, keys):
    return lax.dot_general(queries, keys, (((1,), (1,)), ((), ())), preferred_element_type=f32)


def home_kernel(bias_ref, *refs):
    queries, keys, values = refs[:RING], refs[RING : 2 * RING], refs[2 * RING : 3 * RING]
    summed_ref, lse_ref = refs[-2:]
    bias = bias_ref[8:9, :SLAB]
    lanes = lax.broadcasted_iota(jnp.int32, (SLAB, HEAD), 1)
    ones = jnp.ones((SLAB, HEAD), bf16)
    heads = [slice(h * HEAD, (h + 1) * HEAD) for h in range(GROUP)]
    for pair in ((0, 1), (2, 3)):
        places = [(k, here) for k in pair for here in heads]
        first = keys[0].shape[1] - 2 * WIDE
        scores = [
            dots(queries[k][:, here], keys[k][:, first + here.start : first + here.stop]) + bias
            for k, here in places
        ]
        highest = [jnp.max(block, -1, keepdims=True) for block in scores]
        probs = [jnp.exp2(block - top).astype(bf16) for block, top in zip(scores, highest)]
        start = values[0].shape[1] - WIDE
        both = [
            jnp.dot(
                block,
                jnp.concatenate([values[k][:, start + here.start : start + here.stop], ones], 1),
                preferred_element_type=f32,
            )
            for block, (k, here) in zip(probs, places)
        ]
        for block, (k, here) in zip(both, places):
            summed_ref[:, k * WIDE + here.start : k * WIDE + here.stop] = (
                block[:, :HEAD] / block[:, HEAD:]
            )
        for i, k in enumerate(pair):
            lse = jnp.zeros((SLAB, HEAD), f32)
            for h in range(GROUP):
                n = i * GROUP + h
                lse = jnp.where(lanes == h, highest[n] + jnp.log2(both[n][:, HEAD:]), lse)
            lse_ref[:, k * HEAD : (k + 1) * HEAD] = lse


def at_home(bias, queries, keys, values, token):
    return call(
        home_kernel,
        "at_home",
        [VMEM] * (3 * RING + 1) + [ANY],
        [((SLAB, D), f32, VMEM), ((SLAB, RING * HEAD), f32, VMEM)],
    )(bias, *queries, *keys, *values, token)


def last_keys_kernel(
    place_ref, normed_ref, gains_ref, w_ref, token_ref, o0, o1, o2, o3, cache_ref, held_ref, sems
):
    writes = []
    for part in (1, 2):
        project(normed_ref[...], w_ref, gains_ref, part, held_ref, (part - 1) * D)
        columns = pl.ds((part - 1) * D, D)
        writes.append(
            pltpu.make_async_copy(
                held_ref.at[:, columns], cache_ref.at[:, columns], sems.at[part - 1]
            )
        )
        writes[-1].start()
    dealt(place_ref, held_ref, 2, (o0, o1, o2, o3))
    for write in writes:
        write.wait()


def last_keys(where, normed, gains, w_qkv, token):
    return call(
        last_keys_kernel,
        "last_keys",
        [SMEM] + [VMEM] * 3 + [ANY],
        [((SLAB, 2 * WIDE), bf16, VMEM)] * RING + [((SLAB, 2 * D), bf16, HBM)],
        [pltpu.VMEM((SLAB, 2 * D), bf16), pltpu.SemaphoreType.DMA((2,))],
    )(where, normed, gains, w_qkv, token)


def hold_kernel(*refs):
    pass


def held(array, tokens):
    return call(
        hold_kernel,
        "hold",
        [ANY] * (1 + len(tokens)),
        [(array.shape, array.dtype, ANY)],
        aliases={0: 0},
    )(array, *tokens)[0]


def stack_kernel(*refs):
    blocks, out_ref = refs[:RING], refs[-1]
    first = blocks[0].shape[1] - 2 * WIDE
    for k, block in zip(ORDER, blocks):
        out_ref[k * SLAB : (k + 1) * SLAB, :] = block[:, first:]


def stack(blocks, token, us=0.1):
    return call(
        stack_kernel,
        "stack",
        [VMEM] * RING + [ANY],
        [((RING * SLAB, 2 * WIDE), bf16, VMEM)],
        us=us,
    )(*[blocks[k] for k in ORDER], token)[0]


def attend_kernel(token_ref, *refs, slots):
    n = len(slots)
    queries, olds, bias_ref, outs = refs[:n], refs[n : n + 4], refs[n + 4], refs[n + 5 :]
    lanes = lax.broadcasted_iota(jnp.int32, (SLAB, HEAD), 1)
    ones = jnp.ones((RING * SLAB, HEAD), bf16)
    lse = [jnp.zeros((SLAB, HEAD), f32)] * n
    for h in range(GROUP):
        here = slice(h * HEAD, (h + 1) * HEAD)
        there = slice(WIDE + h * HEAD, WIDE + (h + 1) * HEAD)
        keys = [old[:, here] for old in olds]
        values = [jnp.concatenate([old[:, there], ones], 1) for old in olds]
        joined = [query[:, here] for query in queries]
        joined = jnp.concatenate(joined, 0) if n > 1 else joined[0]
        products = [dots(joined, keys[a]) for a in range(4)]
        for i, slot in enumerate(slots):
            scores = []
            for a in range(4):
                row = a if a else 4 + slot
                scores.append(products[a][i * SLAB : (i + 1) * SLAB] + bias_ref[row : row + 1, :])
            highest = functools.reduce(
                jnp.maximum, [jnp.max(block, -1, keepdims=True) for block in scores]
            )
            both = 0.0
            for a in range(4):
                probs = jnp.exp2(scores[a] - highest).astype(bf16)
                both += jnp.dot(probs, values[a], preferred_element_type=f32)
            total = both[:, HEAD:]
            outs[i][:, here] = (both[:, :HEAD] / total).astype(bf16)
            lse[i] = jnp.where(lanes == h, highest + jnp.log2(total), lse[i])
    for i in range(n):
        rest = lse[i]
        packed = 0.0
        for part in range(3):
            piece = rest.astype(bf16).astype(f32)
            rest = rest - piece
            packed += pltpu.roll(piece, part * GROUP, 1) if part else piece
        outs[i][:, WIDE:] = packed.astype(bf16)


def attend(queries, olds, bias, slots, token):
    return call(
        functools.partial(attend_kernel, slots=slots),
        "attend",
        [ANY] + [VMEM] * (len(slots) + 5),
        [((SLAB, WIDE + HEAD), bf16, VMEM)] * len(slots),
        us=4,
    )(token, *[queries[k] for k in slots], *olds, bias)


def merged(away, summed_ref, lse_ref, k):
    pieces = away[:, WIDE:].astype(f32)
    lse = (
        pieces + pltpu.roll(pieces, HEAD - GROUP, 1) + pltpu.roll(pieces, HEAD - 2 * GROUP, 1)
    )
    share = 1.0 / (1.0 + jnp.exp2(lse_ref[:, k * HEAD : (k + 1) * HEAD] - lse))
    heads = []
    for h in range(GROUP):
        here = slice(k * WIDE + h * HEAD, k * WIDE + (h + 1) * HEAD)
        part = share[:, h : h + 1]
        heads.append(
            part * away[:, h * HEAD : (h + 1) * HEAD].astype(f32)
            + (1.0 - part) * summed_ref[:, here]
        )
    return jnp.concatenate(heads, 1).astype(bf16)


def early_output_kernel(place_ref, a2, a1, a0, w_ref, summed_ref, lse_ref, out_ref):
    total = 0.0
    for k, away in enumerate((a0, a1, a2)):
        weight = w_ref[pl.ds(group_start(place_ref, k), WIDE), :]
        total += jnp.dot(
            merged(away, summed_ref, lse_ref, k), weight, preferred_element_type=f32
        )
    out_ref[...] = total


def early_output(where, away, summed, lse, w_out):
    return call(
        early_output_kernel,
        "early_output",
        [SMEM] + [VMEM] * 6,
        [((SLAB, D), f32, VMEM)],
        us=3,
    )(where, away[2], away[1], away[0], w_out, summed, lse)[0]


def output_kernel(
    place_ref, away, w_ref, summed_ref, lse_ref, early_ref, mixed_ref, gates_ref, out_ref, *edges, row
):
    weight = w_ref[pl.ds(group_start(place_ref, 3), WIDE), :]
    total = early_ref[...] + jnp.dot(
        merged(away, summed_ref, lse_ref, 3), weight, preferred_element_type=f32
    )
    gate = gates_ref[row : row + 1, :]
    out_ref[...] = (mixed_ref[...] + gate * total).astype(bf16)
    if edges:
        for edge_ref, start in zip(edges, edge_starts(place_ref[1])):
            edge_ref[...] = out_ref[pl.ds(start, FRAME), :]


def output(where, away, summed, lse, w_out, early, mixed, gates, row):
    edge = ((FRAME, D), bf16, VMEM)
    return call(
        functools.partial(output_kernel, row=row),
        "output",
        [SMEM] + [VMEM] * 7,
        [((SLAB, D), bf16, VMEM)] + ([edge, edge] if row + 1 < STEPS else []),
    )(where, away[3], w_out, summed, lse, early, mixed, gates)


def sent(block, k):
    return lax.ppermute(block, "patch", ring(k % RING)) if k % RING else block


def shards(latent, stale_kv, timesteps, counts, conv_weight, w_mod, w_qkv, q_gain, k_gain, w_out):
    own_slab = lax.axis_index("patch")
    y, z, c = own_slab // 8, (own_slab // 2) % RING, own_slab % 2
    where = jnp.stack([z, c, timesteps[0], timesteps[1], y]).astype(jnp.int32)
    to_core, to_chip, *pieces = prepare(where, latent, stale_kv)
    chip_rows = lax.ppermute(to_chip, "patch", NEXT_CHIP)
    core_rows = lax.ppermute(to_core, "patch", CORE)
    arrived = {k: sent(pieces[k], k) for k in ORDER}
    old = stack(arrived, arrived[0], us=8)
    old_y = lax.ppermute(old, "patch", ACROSS)
    old_core = lax.ppermute(old, "patch", CORE)
    mod, gains, mixed, *blocks = opening(
        where, latent, core_rows, chip_rows, conv_weight, q_gain, k_gain, w_mod, w_qkv, old
    )
    fresh = {k: sent(blocks[k], k) for k in ORDER}
    gates, bias = aside(where, counts, w_mod, mixed)
    summed, lse = at_home(bias, blocks, blocks, blocks, mixed)
    new = stack(fresh, lse)
    new_y = lax.ppermute(new, "patch", ACROSS)
    new_core = lax.ppermute(new, "patch", CORE)
    old_y = held(old_y, [new])
    olds = [old, old_core, old_y, lax.ppermute(old_y, "patch", CORE)]
    far = attend(fresh, olds, bias, (2, 1), new)
    (near,) = attend(fresh, olds, bias, (3,), far[0])
    (here,) = attend(fresh, olds, bias, (0,), near)
    away = {2: sent(far[0], -2), 1: sent(far[1], -1), 3: sent(near, -3), 0: here}
    early = early_output(where, away, summed, lse, w_out)
    state, to_core, to_chip = output(where, away, summed, lse, w_out, early, mixed, gates, 0)

    chip_rows = lax.ppermute(to_chip, "patch", NEXT_CHIP)
    core_rows = lax.ppermute(to_core, "patch", CORE)
    mixed, normed, *own = next_queries(
        where, state, core_rows, chip_rows, conv_weight, mod, gains, w_qkv, 1
    )
    queries = {k: sent(own[k], k) for k in ORDER}
    new_y = held(new_y, own[:1])
    olds = [new, new_core, new_y, lax.ppermute(new_y, "patch", CORE)]
    *pairs, cache = last_keys(where, normed, gains, w_qkv, normed)
    far = attend(queries, olds, bias, (2, 1), pairs[1])
    (near,) = attend(queries, olds, bias, (3,), far[0])
    (here,) = attend(queries, olds, bias, (0,), near)
    away = {2: sent(far[0], -2), 1: sent(far[1], -1), 3: sent(near, -3), 0: here}
    summed, lse = at_home(bias, own, pairs, pairs, normed)
    early = early_output(where, away, summed, lse, w_out)
    (state,) = output(where, away, summed, lse, w_out, early, mixed, gates, 1)
    return (state, cache)


def solution(mesh):
    rows = P(("req", "patch"), None)
    return jax.shard_map(
        shards,
        mesh=mesh,
        in_specs=(rows, rows, P("req"), P("req"), P(), P(), P(), P(), P(), P()),
        out_specs=(rows, rows),
        check_vma=False,
    )
```

```python
import functools
import math

import jax
import jax.numpy as jnp
from jax import lax
from jax.experimental import pallas as pl
from jax.experimental.pallas import tpu as pltpu
from jax.sharding import PartitionSpec as P

HEAD = 128
FREQ = 256
FRAME = 80
STEPS = 2
SLAB = 128
D = 1536
GROUP = 3
WIDE = GROUP * HEAD
RING = 4
LOG2E = math.log2(math.e)
ORDER = (2, 1, 3, 0)

epsilon = 1e-06
masked_score = -1e30
f32 = jnp.float32
bf16 = jnp.bfloat16


def place(y, z, c):
    return 8 * y + 2 * z + c


DEVICES = [(y, z, c) for y in range(2) for z in range(RING) for c in range(2)]
CORE = [(place(y, z, c), place(y, z, 1 - c)) for y, z, c in DEVICES]
ACROSS = [(place(y, z, c), place(1 - y, z, c)) for y, z, c in DEVICES]


def ring(k):
    return [(place(y, z, c), place(y, (z + k) % RING, c)) for y, z, c in DEVICES]


NEXT_CHIP = [(p, p + 1) for p in range(1, 15, 2)] + [(p + 1, p) for p in range(1, 15, 2)]


VMEM = pl.BlockSpec(memory_space=pltpu.VMEM)
SMEM = pl.BlockSpec(memory_space=pltpu.SMEM)
ANY = pl.BlockSpec(memory_space=pl.ANY)
HBM = pl.BlockSpec(memory_space=pltpu.HBM)


def cost(microseconds):
    return pl.CostEstimate(
        flops=int(microseconds * 1e9), bytes_accessed=int(microseconds * 1e6), transcendentals=0
    )


KEPT = "kept"


def in_vmem(array):
    return pltpu.with_memory_space_constraint(array, pltpu.VMEM)


def in_hbm(array):
    return pltpu.with_memory_space_constraint(array, pltpu.HBM)


def call(body, name, in_specs, outs, scratch=(), aliases=None, megabytes=10, us=0.1):
    return pl.pallas_call(
        body,
        in_specs=in_specs,
        out_specs=[VMEM if spec is KEPT else spec for _, _, spec in outs],
        out_shape=[
            (pltpu.VMEM if spec is KEPT else jax.ShapeDtypeStruct)(shape, dtype)
            for shape, dtype, spec in outs
        ],
        scratch_shapes=list(scratch),
        input_output_aliases=aliases or {},
        compiler_params=pltpu.CompilerParams(vmem_limit_bytes=megabytes * 2**20),
        cost_estimate=cost(us),
        name=name,
    )


def edge_starts(core):
    last = SLAB - FRAME
    return (
        pl.multiple_of(jnp.where(core == 0, last, 0), 16),
        pl.multiple_of(jnp.where(core == 0, 0, last), 16),
    )


def prepare_kernel(place_ref, latent_ref, stale_ref, core_ref, chip_ref, o0, o1, o2, o3, sems):
    outs = (o0, o1, o2, o3)
    core_start, chip_start = edge_starts(place_ref[1])
    copies = [
        pltpu.make_async_copy(latent_ref.at[pl.ds(chip_start, FRAME), :], chip_ref, sems.at[8]),
        pltpu.make_async_copy(latent_ref.at[pl.ds(core_start, FRAME), :], core_ref, sems.at[9]),
    ]
    for k in range(RING):
        start = (place_ref[0] + k) % RING * WIDE
        for part in range(2):
            columns = pl.ds(pl.multiple_of(start + part * D, HEAD), WIDE)
            copies.append(
                pltpu.make_async_copy(
                    stale_ref.at[:, columns],
                    outs[k].at[:, part * WIDE : (part + 1) * WIDE],
                    sems.at[2 * k + part],
                )
            )
    for copy in copies:
        copy.start()
    for copy in copies:
        copy.wait()


def prepare(where, latent, stale_kv):
    edge = ((FRAME, D), bf16, VMEM)
    return call(
        prepare_kernel,
        "prepare",
        [SMEM, HBM, HBM],
        [edge, edge] + [((SLAB, 2 * WIDE), bf16, VMEM)] * RING,
        [pltpu.SemaphoreType.DMA((10,))],
        us=8,
    )(where, in_hbm(latent), in_hbm(stale_kv))


def mix_rows(place_ref, state_ref, core_ref, chip_ref, conv_ref, mod_ref, mixed_ref, normed_ref, row):
    first = place_ref[1] == 0
    state = state_ref[...].astype(f32)
    core_rows = core_ref[...].astype(f32)
    chip_rows = chip_ref[...].astype(f32)
    above = jnp.where(first, chip_rows, core_rows)
    below = jnp.where(first, core_rows, chip_rows)
    before = jnp.concatenate([above, state[: SLAB - FRAME]], 0)
    after_rows = jnp.concatenate([state[FRAME:], below], 0)
    mixed = (
        state
        + conv_ref[0:1, :] * before
        + conv_ref[1:2, :] * state
        + conv_ref[2:3, :] * after_rows
    )
    mixed_ref[...] = mixed
    shift = mod_ref[row : row + 1, :D]
    scale = mod_ref[row : row + 1, D : 2 * D]
    centred = mixed - jnp.mean(mixed, -1, keepdims=True)
    variance = jnp.mean(centred * centred, -1, keepdims=True)
    normed_ref[...] = (centred * lax.rsqrt(variance + epsilon) * (1.0 + scale) + shift).astype(bf16)


def embedding(moment):
    halfway = FREQ // 2
    index = lax.broadcasted_iota(jnp.int32, (halfway, 1), 0).astype(f32)
    angles = moment.astype(f32) * jnp.exp(-math.log(10000.0) * index / halfway)
    values = jnp.concatenate([jnp.cos(angles), jnp.sin(angles)], 0)
    return values / (1.0 + jnp.exp(-values))


def head_normed(block, gain):
    mean_square = jnp.mean(block * block, -1, keepdims=True)
    return (block * lax.rsqrt(mean_square + epsilon) * gain).astype(bf16)


def normed_heads(normed, weight, gain_ref, row, group, out_ref, start):
    block = jnp.dot(normed, weight, preferred_element_type=f32)
    gain = gain_ref[row : row + 1, pl.ds(group, WIDE)]
    for h in range(GROUP):
        here = slice(h * HEAD, (h + 1) * HEAD)
        out_ref[:, start + h * HEAD : start + (h + 1) * HEAD] = head_normed(
            block[:, here], gain[:, here]
        )


def group_start(place_ref, k):
    return pl.multiple_of((place_ref[0] + k) % RING * WIDE, HEAD)


def project(normed, w_ref, gains_ref, part, held_ref, first):
    block = jnp.dot(normed, w_ref[:, part * D : (part + 1) * D], preferred_element_type=f32)
    if part == 2:
        held_ref[:, first : first + D] = block.astype(bf16)
        return
    for h in range(D // HEAD):
        here = slice(h * HEAD, (h + 1) * HEAD)
        held_ref[:, first + here.start : first + here.stop] = head_normed(
            block[:, here], gains_ref[part : part + 1, here]
        )


def dealt(place_ref, held_ref, parts, outs):
    for k, out_ref in enumerate(outs):
        for i in range(parts):
            start = pl.multiple_of(group_start(place_ref, k) + i * D, HEAD)
            out_ref[:, i * WIDE : (i + 1) * WIDE] = held_ref[:, pl.ds(start, WIDE)]


def modulated(active, weights):
    return [jnp.sum(weights * active[s], 0, keepdims=True) for s in range(STEPS)]


def open_kernel(
    place_ref, latent_ref, core_ref, chip_ref, taps_ref, q_gain_ref, k_gain_ref, w_mod_ref,
    w_qkv_ref, token_ref, mod_ref, gains_ref, mixed_ref, o0, o1, o2, o3,
    state_ref, conv_ref, q_held, k_held, normed_ref, held_ref, sems
):
    copies = [
        pltpu.make_async_copy(latent_ref, state_ref, sems.at[0]),
        pltpu.make_async_copy(taps_ref, conv_ref, sems.at[1]),
        pltpu.make_async_copy(q_gain_ref, q_held, sems.at[2]),
        pltpu.make_async_copy(k_gain_ref, k_held, sems.at[3]),
    ]
    for copy in copies:
        copy.start()
    active = [embedding(place_ref[2 + s]) for s in range(STEPS)]
    for i in range(4):
        here = slice(i * 2 * D // 4, (i + 1) * 2 * D // 4)
        for s, row in enumerate(modulated(active, w_mod_ref[:, here])):
            mod_ref[s : s + 1, here] = row
    for copy in copies:
        copy.wait()
    gains_ref[0:1, :] = (q_held[...] * (LOG2E / math.sqrt(HEAD))).reshape(1, D)
    gains_ref[1:2, :] = k_held[...].reshape(1, D)
    mix_rows(place_ref, state_ref, core_ref, chip_ref, conv_ref, mod_ref, mixed_ref, normed_ref, 0)
    for part in range(3):
        project(normed_ref[...], w_qkv_ref, gains_ref, part, held_ref, part * D)
    dealt(place_ref, held_ref, 3, (o0, o1, o2, o3))


def opening(where, state, core_rows, chip_rows, conv_weight, q_gain, k_gain, w_mod, w_qkv, token):
    return call(
        open_kernel,
        "opening",
        [SMEM, HBM, VMEM, VMEM] + [HBM] * 3 + [VMEM] * 2 + [ANY],
        [((STEPS, 2 * D), f32, VMEM), ((2, D), f32, VMEM), ((SLAB, D), f32, VMEM)]
        + [((SLAB, 3 * WIDE), bf16, VMEM)] * RING,
        [
            pltpu.VMEM((SLAB, D), bf16),
            pltpu.VMEM((3, D), f32),
            pltpu.VMEM((D,), f32),
            pltpu.VMEM((D,), f32),
            pltpu.VMEM((SLAB, D), bf16),
            pltpu.VMEM((SLAB, 3 * D), bf16),
            pltpu.SemaphoreType.DMA((4,)),
        ],
        us=10,
    )(
        where, in_hbm(state), core_rows, chip_rows, in_hbm(conv_weight), in_hbm(q_gain),
        in_hbm(k_gain), w_mod, w_qkv, token,
    )


def fill_bias(place_ref, counts_ref, bias_ref):
    z, c, y = place_ref[0], place_ref[1], place_ref[4]
    index = lax.broadcasted_iota(jnp.int32, (1, SLAB), 1)
    for a, (yy, cc) in enumerate(((y, c), (y, 1 - c), (1 - y, c), (1 - y, 1 - c))):
        for j in range(RING):
            slab = 8 * yy + 2 * ((z + RING - j) % RING) + cc
            here = slice(j * SLAB, (j + 1) * SLAB)
            row = jnp.where(index < counts_ref[slab], 0.0, masked_score)
            bias_ref[a : a + 1, here] = row
            if a == 0:
                for slot in range(RING):
                    bias_ref[4 + slot : 5 + slot, here] = (
                        jnp.full((1, SLAB), masked_score, f32) if slot == j else row
                    )
                if j == 0:
                    bias_ref[8:9, here] = row


def aside_kernel(place_ref, counts_ref, w_mod_ref, token_ref, gates_ref, bias_ref, held, sem):
    load = pltpu.make_async_copy(w_mod_ref.at[:, 2 * D :], held, sem)
    load.start()
    active = [embedding(place_ref[2 + s]) for s in range(STEPS)]
    fill_bias(place_ref, counts_ref, bias_ref)
    load.wait()
    for s, row in enumerate(modulated(active, held[...])):
        gates_ref[s : s + 1, :] = row


def aside(where, counts, w_mod, token):
    return call(
        aside_kernel,
        "aside",
        [SMEM, SMEM, HBM, ANY],
        [((STEPS, D), f32, VMEM), ((16, RING * SLAB), f32, VMEM)],
        [pltpu.VMEM((FREQ, D), f32), pltpu.SemaphoreType.DMA],
    )(where, counts, in_hbm(w_mod), token)


def next_kernel(
    place_ref, state_ref, core_ref, chip_ref, conv_ref, mod_ref, gains_ref, w_qkv_ref,
    mixed_ref, normed_ref, o0, o1, o2, o3, held_ref, *, row
):
    mix_rows(
        place_ref, state_ref, core_ref, chip_ref, conv_ref, mod_ref, mixed_ref, normed_ref, row
    )
    project(normed_ref[...], w_qkv_ref, gains_ref, 0, held_ref, 0)
    dealt(place_ref, held_ref, 1, (o0, o1, o2, o3))


def next_queries(where, state, core_rows, chip_rows, conv_weight, mod, gains, w_qkv, row):
    return call(
        functools.partial(next_kernel, row=row),
        "next_queries",
        [SMEM] + [VMEM] * 7,
        [((SLAB, D), f32, VMEM), ((SLAB, D), bf16, VMEM)] + [((SLAB, WIDE), bf16, VMEM)] * RING,
        [pltpu.VMEM((SLAB, D), bf16)],
    )(where, state, core_rows, chip_rows, conv_weight, mod, gains, w_qkv)


def dots(queries, keys):
    return lax.dot_general(queries, keys, (((1,), (1,)), ((), ())), preferred_element_type=f32)


def home_kernel(bias_ref, *refs):
    queries, keys, values = refs[:RING], refs[RING : 2 * RING], refs[2 * RING : 3 * RING]
    summed_ref, lse_ref = refs[-2:]
    bias = bias_ref[8:9, :SLAB]
    lanes = lax.broadcasted_iota(jnp.int32, (SLAB, HEAD), 1)
    ones = jnp.ones((SLAB, HEAD), bf16)
    heads = [slice(h * HEAD, (h + 1) * HEAD) for h in range(GROUP)]
    for pair in ((0, 1), (2, 3)):
        places = [(k, here) for k in pair for here in heads]
        first = keys[0].shape[1] - 2 * WIDE
        scores = [
            dots(queries[k][:, here], keys[k][:, first + here.start : first + here.stop]) + bias
            for k, here in places
        ]
        highest = [jnp.max(block, -1, keepdims=True) for block in scores]
        probs = [jnp.exp2(block - top).astype(bf16) for block, top in zip(scores, highest)]
        start = values[0].shape[1] - WIDE
        both = [
            jnp.dot(
                block,
                jnp.concatenate([values[k][:, start + here.start : start + here.stop], ones], 1),
                preferred_element_type=f32,
            )
            for block, (k, here) in zip(probs, places)
        ]
        for block, (k, here) in zip(both, places):
            summed_ref[:, k * WIDE + here.start : k * WIDE + here.stop] = (
                block[:, :HEAD] / block[:, HEAD:]
            )
        for i, k in enumerate(pair):
            lse = jnp.zeros((SLAB, HEAD), f32)
            for h in range(GROUP):
                n = i * GROUP + h
                lse = jnp.where(lanes == h, highest[n] + jnp.log2(both[n][:, HEAD:]), lse)
            lse_ref[:, k * HEAD : (k + 1) * HEAD] = lse


def at_home(bias, queries, keys, values, token):
    return call(
        home_kernel,
        "at_home",
        [VMEM] * (3 * RING + 1) + [ANY],
        [((SLAB, D), f32, VMEM), ((SLAB, RING * HEAD), f32, VMEM)],
    )(bias, *queries, *keys, *values, token)


def last_keys_kernel(
    place_ref, normed_ref, gains_ref, w_ref, token_ref, o0, o1, o2, o3, cache_ref, held_ref, sems
):
    writes = []
    for part in (1, 2):
        project(normed_ref[...], w_ref, gains_ref, part, held_ref, (part - 1) * D)
        columns = pl.ds((part - 1) * D, D)
        writes.append(
            pltpu.make_async_copy(
                held_ref.at[:, columns], cache_ref.at[:, columns], sems.at[part - 1]
            )
        )
        writes[-1].start()
    dealt(place_ref, held_ref, 2, (o0, o1, o2, o3))
    for write in writes:
        write.wait()


def last_keys(where, normed, gains, w_qkv, token):
    return call(
        last_keys_kernel,
        "last_keys",
        [SMEM] + [VMEM] * 3 + [ANY],
        [((SLAB, 2 * WIDE), bf16, VMEM)] * RING + [((SLAB, 2 * D), bf16, HBM)],
        [pltpu.VMEM((SLAB, 2 * D), bf16), pltpu.SemaphoreType.DMA((2,))],
    )(where, normed, gains, w_qkv, token)


def hold_kernel(*refs):
    pass


def held(array, tokens):
    return call(
        hold_kernel,
        "hold",
        [ANY] * (1 + len(tokens)),
        [(array.shape, array.dtype, ANY)],
        aliases={0: 0},
    )(array, *tokens)[0]


def stack_kernel(*refs):
    blocks, out_ref = refs[:RING], refs[-1]
    first = blocks[0].shape[1] - 2 * WIDE
    for k, block in zip(ORDER, blocks):
        out_ref[k * SLAB : (k + 1) * SLAB, :] = block[:, first:]


def stack(blocks, token, us=0.1):
    return call(
        stack_kernel,
        "stack",
        [VMEM] * RING + [ANY],
        [((RING * SLAB, 2 * WIDE), bf16, VMEM)],
        us=us,
    )(*[blocks[k] for k in ORDER], token)[0]


def attend_kernel(token_ref, *refs, slots):
    n = len(slots)
    queries, olds, bias_ref, outs = refs[:n], refs[n : n + 4], refs[n + 4], refs[n + 5 :]
    lanes = lax.broadcasted_iota(jnp.int32, (SLAB, HEAD), 1)
    ones = jnp.ones((RING * SLAB, HEAD), bf16)
    lse = [jnp.zeros((SLAB, HEAD), f32)] * n
    for h in range(GROUP):
        here = slice(h * HEAD, (h + 1) * HEAD)
        there = slice(WIDE + h * HEAD, WIDE + (h + 1) * HEAD)
        keys = [old[:, here] for old in olds]
        values = [jnp.concatenate([old[:, there], ones], 1) for old in olds]
        joined = [query[:, here] for query in queries]
        joined = jnp.concatenate(joined, 0) if n > 1 else joined[0]
        products = [dots(joined, keys[a]) for a in range(4)]
        for i, slot in enumerate(slots):
            scores = []
            for a in range(4):
                row = a if a else 4 + slot
                scores.append(products[a][i * SLAB : (i + 1) * SLAB] + bias_ref[row : row + 1, :])
            highest = functools.reduce(
                jnp.maximum, [jnp.max(block, -1, keepdims=True) for block in scores]
            )
            both = 0.0
            for a in range(4):
                probs = jnp.exp2(scores[a] - highest).astype(bf16)
                both += jnp.dot(probs, values[a], preferred_element_type=f32)
            total = both[:, HEAD:]
            outs[i][:, here] = (both[:, :HEAD] / total).astype(bf16)
            lse[i] = jnp.where(lanes == h, highest + jnp.log2(total), lse[i])
    for i in range(n):
        rest = lse[i]
        packed = 0.0
        for part in range(3):
            piece = rest.astype(bf16).astype(f32)
            rest = rest - piece
            packed += pltpu.roll(piece, part * GROUP, 1) if part else piece
        outs[i][:, WIDE:] = packed.astype(bf16)


def attend(queries, olds, bias, slots, token):
    return call(
        functools.partial(attend_kernel, slots=slots),
        "attend",
        [ANY] + [VMEM] * (len(slots) + 5),
        [((SLAB, WIDE + HEAD), bf16, VMEM)] * len(slots),
        us=4,
    )(token, *[queries[k] for k in slots], *olds, bias)


def merged(away, summed_ref, lse_ref, k):
    pieces = away[:, WIDE:].astype(f32)
    lse = (
        pieces + pltpu.roll(pieces, HEAD - GROUP, 1) + pltpu.roll(pieces, HEAD - 2 * GROUP, 1)
    )
    share = 1.0 / (1.0 + jnp.exp2(lse_ref[:, k * HEAD : (k + 1) * HEAD] - lse))
    heads = []
    for h in range(GROUP):
        here = slice(k * WIDE + h * HEAD, k * WIDE + (h + 1) * HEAD)
        part = share[:, h : h + 1]
        heads.append(
            part * away[:, h * HEAD : (h + 1) * HEAD].astype(f32)
            + (1.0 - part) * summed_ref[:, here]
        )
    return jnp.concatenate(heads, 1).astype(bf16)


def early_output_kernel(place_ref, a2, a1, a0, w_ref, summed_ref, lse_ref, out_ref):
    total = 0.0
    for k, away in enumerate((a0, a1, a2)):
        weight = w_ref[pl.ds(group_start(place_ref, k), WIDE), :]
        total += jnp.dot(
            merged(away, summed_ref, lse_ref, k), weight, preferred_element_type=f32
        )
    out_ref[...] = total


def early_output(where, away, summed, lse, w_out):
    return call(
        early_output_kernel,
        "early_output",
        [SMEM] + [VMEM] * 6,
        [((SLAB, D), f32, VMEM)],
        us=3,
    )(where, away[2], away[1], away[0], w_out, summed, lse)[0]


def output_kernel(
    place_ref, away, w_ref, summed_ref, lse_ref, early_ref, mixed_ref, gates_ref, out_ref, *edges, row
):
    weight = w_ref[pl.ds(group_start(place_ref, 3), WIDE), :]
    total = early_ref[...] + jnp.dot(
        merged(away, summed_ref, lse_ref, 3), weight, preferred_element_type=f32
    )
    gate = gates_ref[row : row + 1, :]
    out_ref[...] = (mixed_ref[...] + gate * total).astype(bf16)
    for edge_ref, start in zip(edges, edge_starts(place_ref[1])):
        edge_ref[...] = out_ref[pl.ds(start, FRAME), :]


def output(where, away, summed, lse, w_out, early, mixed, gates, row):
    edge = ((FRAME, D), bf16, VMEM)
    return call(
        functools.partial(output_kernel, row=row),
        "output",
        [SMEM] + [VMEM] * 7,
        [((SLAB, D), bf16, VMEM), edge, edge],
    )(where, away[3], w_out, summed, lse, early, mixed, gates)


def last_output_kernel(
    place_ref, away, w_ref, summed_ref, lse_ref, early_ref, mixed_ref, gates_ref, out_ref,
    held_ref, sems, *, row
):
    attended = merged(away, summed_ref, lse_ref, 3)
    rows = pl.ds(group_start(place_ref, 3), WIDE)
    width = D // 3
    writes = []
    for i in range(3):
        here = slice(i * width, (i + 1) * width)
        total = early_ref[:, here] + jnp.dot(
            attended, w_ref[rows, here], preferred_element_type=f32
        )
        gate = gates_ref[row : row + 1, here]
        held_ref[:, here] = (mixed_ref[:, here] + gate * total).astype(bf16)
        writes.append(
            pltpu.make_async_copy(held_ref.at[:, here], out_ref.at[:, here], sems.at[i])
        )
        writes[-1].start()
    for write in writes:
        write.wait()


def last_output(where, away, summed, lse, w_out, early, mixed, gates, row):
    return call(
        functools.partial(last_output_kernel, row=row),
        "last_output",
        [SMEM] + [VMEM] * 7,
        [((SLAB, D), bf16, HBM)],
        [pltpu.VMEM((SLAB, D), bf16), pltpu.SemaphoreType.DMA((3,))],
    )(where, away[3], w_out, summed, lse, early, mixed, gates)[0]


def sent(block, k):
    return lax.ppermute(block, "patch", ring(k % RING)) if k % RING else block


def shards(latent, stale_kv, timesteps, counts, conv_weight, w_mod, w_qkv, q_gain, k_gain, w_out):
    own_slab = lax.axis_index("patch")
    y, z, c = own_slab // 8, (own_slab // 2) % RING, own_slab % 2
    where = jnp.stack([z, c, timesteps[0], timesteps[1], y]).astype(jnp.int32)
    to_core, to_chip, *pieces = prepare(where, latent, stale_kv)
    chip_rows = lax.ppermute(to_chip, "patch", NEXT_CHIP)
    core_rows = lax.ppermute(to_core, "patch", CORE)
    arrived = {k: sent(pieces[k], k) for k in ORDER}
    old = stack(arrived, arrived[0], us=8)
    old_y = lax.ppermute(old, "patch", ACROSS)
    old_core = lax.ppermute(old, "patch", CORE)
    mod, gains, mixed, *blocks = opening(
        where, latent, core_rows, chip_rows, conv_weight, q_gain, k_gain, w_mod, w_qkv, old
    )
    fresh = {k: sent(blocks[k], k) for k in ORDER}
    gates, bias = aside(where, counts, w_mod, mixed)
    summed, lse = at_home(bias, blocks, blocks, blocks, mixed)
    new = stack(fresh, lse)
    new_y = lax.ppermute(new, "patch", ACROSS)
    new_core = lax.ppermute(new, "patch", CORE)
    old_y = held(old_y, [fresh[2], fresh[1], fresh[3], lse])
    olds = [old, old_core, old_y, lax.ppermute(old_y, "patch", CORE)]
    far = attend(fresh, olds, bias, (2, 1), new)
    (near,) = attend(fresh, olds, bias, (3,), far[0])
    (here,) = attend(fresh, olds, bias, (0,), near)
    away = {2: sent(far[0], -2), 1: sent(far[1], -1), 3: sent(near, -3), 0: here}
    early = early_output(where, away, summed, lse, w_out)
    state, to_core, to_chip = output(where, away, summed, lse, w_out, early, mixed, gates, 0)

    chip_rows = lax.ppermute(to_chip, "patch", NEXT_CHIP)
    core_rows = lax.ppermute(to_core, "patch", CORE)
    mixed, normed, *own = next_queries(
        where, state, core_rows, chip_rows, conv_weight, mod, gains, w_qkv, 1
    )
    queries = {k: sent(own[k], k) for k in ORDER}
    new_y = held(new_y, own[:1])
    olds = [new, new_core, new_y, lax.ppermute(new_y, "patch", CORE)]
    *pairs, cache = last_keys(where, normed, gains, w_qkv, normed)
    far = attend(queries, olds, bias, (2, 1), pairs[1])
    (near,) = attend(queries, olds, bias, (3,), far[0])
    (here,) = attend(queries, olds, bias, (0,), near)
    away = {2: sent(far[0], -2), 1: sent(far[1], -1), 3: sent(near, -3), 0: here}
    summed, lse = at_home(bias, own, pairs, pairs, normed)
    early = early_output(where, away, summed, lse, w_out)
    state = last_output(where, away, summed, lse, w_out, early, mixed, gates, 1)
    return (state, cache)


def solution(mesh):
    rows = P(("req", "patch"), None)
    return jax.shard_map(
        shards,
        mesh=mesh,
        in_specs=(rows, rows, P("req"), P("req"), P(), P(), P(), P(), P(), P()),
        out_specs=(rows, rows),
        check_vma=False,
    )
```

```python
import functools
import math

import jax
import jax.numpy as jnp
from jax import lax
from jax.experimental import pallas as pl
from jax.experimental.pallas import tpu as pltpu
from jax.sharding import PartitionSpec as P

HEAD = 128
FREQ = 256
FRAME = 80
STEPS = 2
SLAB = 128
D = 1536
GROUP = 3
WIDE = GROUP * HEAD
RING = 4
LOG2E = math.log2(math.e)
EXTRA = 16
ORDER = (2, 1, 3, 0)

epsilon = 1e-06
masked_score = -1e30
f32 = jnp.float32
bf16 = jnp.bfloat16


def place(y, z, c):
    return 8 * y + 2 * z + c


DEVICES = [(y, z, c) for y in range(2) for z in range(RING) for c in range(2)]
CORE = [(place(y, z, c), place(y, z, 1 - c)) for y, z, c in DEVICES]
ACROSS = [(place(y, z, c), place(1 - y, z, c)) for y, z, c in DEVICES]


def ring(k):
    return [(place(y, z, c), place(y, (z + k) % RING, c)) for y, z, c in DEVICES]


NEXT_CHIP = [(p, p + 1) for p in range(1, 15, 2)] + [(p + 1, p) for p in range(1, 15, 2)]


VMEM = pl.BlockSpec(memory_space=pltpu.VMEM)
SMEM = pl.BlockSpec(memory_space=pltpu.SMEM)
ANY = pl.BlockSpec(memory_space=pl.ANY)
HBM = pl.BlockSpec(memory_space=pltpu.HBM)


def cost(microseconds):
    return pl.CostEstimate(
        flops=int(microseconds * 1e9), bytes_accessed=int(microseconds * 1e6), transcendentals=0
    )


KEPT = "kept"


def in_vmem(array):
    return pltpu.with_memory_space_constraint(array, pltpu.VMEM)


def in_hbm(array):
    return pltpu.with_memory_space_constraint(array, pltpu.HBM)


def call(body, name, in_specs, outs, scratch=(), aliases=None, megabytes=10, us=0.1):
    return pl.pallas_call(
        body,
        in_specs=in_specs,
        out_specs=[VMEM if spec is KEPT else spec for _, _, spec in outs],
        out_shape=[
            (pltpu.VMEM if spec is KEPT else jax.ShapeDtypeStruct)(shape, dtype)
            for shape, dtype, spec in outs
        ],
        scratch_shapes=list(scratch),
        input_output_aliases=aliases or {},
        compiler_params=pltpu.CompilerParams(vmem_limit_bytes=megabytes * 2**20),
        cost_estimate=cost(us),
        name=name,
    )


def edge_starts(core):
    last = SLAB - FRAME
    return (
        pl.multiple_of(jnp.where(core == 0, last, 0), 16),
        pl.multiple_of(jnp.where(core == 0, 0, last), 16),
    )


def prepare_kernel(place_ref, latent_ref, stale_ref, core_ref, chip_ref, o0, o1, o2, o3, sems):
    outs = (o0, o1, o2, o3)
    core_start, chip_start = edge_starts(place_ref[1])
    copies = [
        pltpu.make_async_copy(latent_ref.at[pl.ds(chip_start, FRAME), :], chip_ref, sems.at[8]),
        pltpu.make_async_copy(latent_ref.at[pl.ds(core_start, FRAME), :], core_ref, sems.at[9]),
    ]
    for k in range(RING):
        start = (place_ref[0] + k) % RING * WIDE
        for part in range(2):
            columns = pl.ds(pl.multiple_of(start + part * D, HEAD), WIDE)
            copies.append(
                pltpu.make_async_copy(
                    stale_ref.at[:, columns],
                    outs[k].at[:, part * WIDE : (part + 1) * WIDE],
                    sems.at[2 * k + part],
                )
            )
    for copy in copies:
        copy.start()
    for copy in copies:
        copy.wait()


def prepare(where, latent, stale_kv):
    edge = ((FRAME, D), bf16, VMEM)
    return call(
        prepare_kernel,
        "prepare",
        [SMEM, HBM, HBM],
        [edge, edge] + [((SLAB, 2 * WIDE), bf16, VMEM)] * RING,
        [pltpu.SemaphoreType.DMA((10,))],
        us=8,
    )(where, in_hbm(latent), in_hbm(stale_kv))


def mix_rows(place_ref, state_ref, core_ref, chip_ref, conv_ref, mod_ref, mixed_ref, normed_ref, row):
    first = place_ref[1] == 0
    state = state_ref[...].astype(f32)
    core_rows = core_ref[...].astype(f32)
    chip_rows = chip_ref[...].astype(f32)
    above = jnp.where(first, chip_rows, core_rows)
    below = jnp.where(first, core_rows, chip_rows)
    before = jnp.concatenate([above, state[: SLAB - FRAME]], 0)
    after_rows = jnp.concatenate([state[FRAME:], below], 0)
    mixed = (
        state
        + conv_ref[0:1, :] * before
        + conv_ref[1:2, :] * state
        + conv_ref[2:3, :] * after_rows
    )
    mixed_ref[...] = mixed
    shift = mod_ref[row : row + 1, :D]
    scale = mod_ref[row : row + 1, D : 2 * D]
    centred = mixed - jnp.mean(mixed, -1, keepdims=True)
    variance = jnp.mean(centred * centred, -1, keepdims=True)
    normed_ref[...] = (centred * lax.rsqrt(variance + epsilon) * (1.0 + scale) + shift).astype(bf16)


def embedding(moment):
    halfway = FREQ // 2
    index = lax.broadcasted_iota(jnp.int32, (halfway, 1), 0).astype(f32)
    angles = moment.astype(f32) * jnp.exp(-math.log(10000.0) * index / halfway)
    values = jnp.concatenate([jnp.cos(angles), jnp.sin(angles)], 0)
    return values / (1.0 + jnp.exp(-values))


def head_normed(block, gain):
    mean_square = jnp.mean(block * block, -1, keepdims=True)
    return (block * lax.rsqrt(mean_square + epsilon) * gain).astype(bf16)


def normed_heads(normed, weight, gain_ref, row, group, out_ref, start):
    block = jnp.dot(normed, weight, preferred_element_type=f32)
    gain = gain_ref[row : row + 1, pl.ds(group, WIDE)]
    for h in range(GROUP):
        here = slice(h * HEAD, (h + 1) * HEAD)
        out_ref[:, start + h * HEAD : start + (h + 1) * HEAD] = head_normed(
            block[:, here], gain[:, here]
        )


def group_start(place_ref, k):
    return pl.multiple_of((place_ref[0] + k) % RING * WIDE, HEAD)


def project(normed, w_ref, gains_ref, part, held_ref, first):
    block = jnp.dot(normed, w_ref[:, part * D : (part + 1) * D], preferred_element_type=f32)
    if part == 2:
        held_ref[:, first : first + D] = block.astype(bf16)
        return
    for h in range(D // HEAD):
        here = slice(h * HEAD, (h + 1) * HEAD)
        held_ref[:, first + here.start : first + here.stop] = head_normed(
            block[:, here], gains_ref[part : part + 1, here]
        )


def dealt(place_ref, held_ref, parts, outs):
    for k, out_ref in enumerate(outs):
        for i in range(parts):
            start = pl.multiple_of(group_start(place_ref, k) + i * D, HEAD)
            out_ref[:, i * WIDE : (i + 1) * WIDE] = held_ref[:, pl.ds(start, WIDE)]


def modulated(active, weights):
    return [jnp.sum(weights * active[s], 0, keepdims=True) for s in range(STEPS)]


def open_kernel(
    place_ref, latent_ref, core_ref, chip_ref, taps_ref, q_gain_ref, k_gain_ref, w_mod_ref,
    w_qkv_ref, token_ref, mod_ref, gains_ref, mixed_ref, o0, o1, o2, o3,
    state_ref, conv_ref, q_held, k_held, normed_ref, held_ref, sems
):
    copies = [
        pltpu.make_async_copy(latent_ref, state_ref, sems.at[0]),
        pltpu.make_async_copy(taps_ref, conv_ref, sems.at[1]),
        pltpu.make_async_copy(q_gain_ref, q_held, sems.at[2]),
        pltpu.make_async_copy(k_gain_ref, k_held, sems.at[3]),
    ]
    for copy in copies:
        copy.start()
    active = [embedding(place_ref[2 + s]) for s in range(STEPS)]
    for i in range(4):
        here = slice(i * 2 * D // 4, (i + 1) * 2 * D // 4)
        for s, row in enumerate(modulated(active, w_mod_ref[:, here])):
            mod_ref[s : s + 1, here] = row
    for copy in copies:
        copy.wait()
    gains_ref[0:1, :] = (q_held[...] * (LOG2E / math.sqrt(HEAD))).reshape(1, D)
    gains_ref[1:2, :] = k_held[...].reshape(1, D)
    mix_rows(place_ref, state_ref, core_ref, chip_ref, conv_ref, mod_ref, mixed_ref, normed_ref, 0)
    for part in range(3):
        project(normed_ref[...], w_qkv_ref, gains_ref, part, held_ref, part * D)
    dealt(place_ref, held_ref, 3, (o0, o1, o2, o3))


def opening(where, state, core_rows, chip_rows, conv_weight, q_gain, k_gain, w_mod, w_qkv, token):
    return call(
        open_kernel,
        "opening",
        [SMEM, HBM, VMEM, VMEM] + [HBM] * 3 + [VMEM] * 2 + [ANY],
        [((STEPS, 2 * D), f32, VMEM), ((2, D), f32, VMEM), ((SLAB, D), f32, VMEM)]
        + [((SLAB, 3 * WIDE), bf16, VMEM)] * RING,
        [
            pltpu.VMEM((SLAB, D), bf16),
            pltpu.VMEM((3, D), f32),
            pltpu.VMEM((D,), f32),
            pltpu.VMEM((D,), f32),
            pltpu.VMEM((SLAB, D), bf16),
            pltpu.VMEM((SLAB, 3 * D), bf16),
            pltpu.SemaphoreType.DMA((4,)),
        ],
        us=10,
    )(
        where, in_hbm(state), core_rows, chip_rows, in_hbm(conv_weight), in_hbm(q_gain),
        in_hbm(k_gain), w_mod, w_qkv, token,
    )


def fill_bias(place_ref, counts_ref, bias_ref):
    z, c, y = place_ref[0], place_ref[1], place_ref[4]
    index = lax.broadcasted_iota(jnp.int32, (1, SLAB), 1)
    for a, (yy, cc) in enumerate(((y, c), (y, 1 - c), (1 - y, c), (1 - y, 1 - c))):
        for j in range(RING):
            slab = 8 * yy + 2 * ((z + RING - j) % RING) + cc
            here = slice(j * SLAB, (j + 1) * SLAB)
            row = jnp.where(index < counts_ref[slab], 0.0, masked_score)
            bias_ref[a : a + 1, here] = row
            if a == 0:
                for slot in range(RING):
                    bias_ref[4 + slot : 5 + slot, here] = (
                        jnp.full((1, SLAB), masked_score, f32) if slot == j else row
                    )
                if j == 0:
                    bias_ref[8:9, here] = row


def aside_kernel(place_ref, counts_ref, w_mod_ref, token_ref, gates_ref, bias_ref, held, sem):
    load = pltpu.make_async_copy(w_mod_ref.at[:, 2 * D :], held, sem)
    load.start()
    active = [embedding(place_ref[2 + s]) for s in range(STEPS)]
    fill_bias(place_ref, counts_ref, bias_ref)
    load.wait()
    for s, row in enumerate(modulated(active, held[...])):
        gates_ref[s : s + 1, :] = row


def aside(where, counts, w_mod, token):
    return call(
        aside_kernel,
        "aside",
        [SMEM, SMEM, HBM, ANY],
        [((STEPS, D), f32, VMEM), ((16, RING * SLAB), f32, VMEM)],
        [pltpu.VMEM((FREQ, D), f32), pltpu.SemaphoreType.DMA],
    )(where, counts, in_hbm(w_mod), token)


def next_kernel(
    place_ref, state_ref, core_ref, chip_ref, conv_ref, mod_ref, gains_ref, w_qkv_ref,
    mixed_ref, normed_ref, o0, o1, o2, o3, held_ref, *, row
):
    mix_rows(
        place_ref, state_ref, core_ref, chip_ref, conv_ref, mod_ref, mixed_ref, normed_ref, row
    )
    project(normed_ref[...], w_qkv_ref, gains_ref, 0, held_ref, 0)
    dealt(place_ref, held_ref, 1, (o0, o1, o2, o3))


def next_queries(where, state, core_rows, chip_rows, conv_weight, mod, gains, w_qkv, row):
    return call(
        functools.partial(next_kernel, row=row),
        "next_queries",
        [SMEM] + [VMEM] * 7,
        [((SLAB, D), f32, VMEM), ((SLAB, D), bf16, VMEM)] + [((SLAB, WIDE), bf16, VMEM)] * RING,
        [pltpu.VMEM((SLAB, D), bf16)],
    )(where, state, core_rows, chip_rows, conv_weight, mod, gains, w_qkv)


def dots(queries, keys):
    return lax.dot_general(queries, keys, (((1,), (1,)), ((), ())), preferred_element_type=f32)


def home_kernel(bias_ref, *refs):
    queries, keys, values = refs[:RING], refs[RING : 2 * RING], refs[2 * RING : 3 * RING]
    summed_ref, lse_ref = refs[-2:]
    bias = bias_ref[8:9, :SLAB]
    lanes = lax.broadcasted_iota(jnp.int32, (SLAB, HEAD), 1)
    ones = jnp.ones((SLAB, HEAD), bf16)
    heads = [slice(h * HEAD, (h + 1) * HEAD) for h in range(GROUP)]
    for pair in ((0, 1), (2, 3)):
        places = [(k, here) for k in pair for here in heads]
        first = keys[0].shape[1] - 2 * WIDE
        scores = [
            dots(queries[k][:, here], keys[k][:, first + here.start : first + here.stop]) + bias
            for k, here in places
        ]
        highest = [jnp.max(block, -1, keepdims=True) for block in scores]
        probs = [jnp.exp2(block - top).astype(bf16) for block, top in zip(scores, highest)]
        start = values[0].shape[1] - WIDE
        both = [
            jnp.dot(
                block,
                jnp.concatenate([values[k][:, start + here.start : start + here.stop], ones], 1),
                preferred_element_type=f32,
            )
            for block, (k, here) in zip(probs, places)
        ]
        for block, (k, here) in zip(both, places):
            summed_ref[:, k * WIDE + here.start : k * WIDE + here.stop] = (
                block[:, :HEAD] / block[:, HEAD:]
            )
        for i, k in enumerate(pair):
            lse = jnp.zeros((SLAB, HEAD), f32)
            for h in range(GROUP):
                n = i * GROUP + h
                lse = jnp.where(lanes == h, highest[n] + jnp.log2(both[n][:, HEAD:]), lse)
            lse_ref[:, k * HEAD : (k + 1) * HEAD] = lse


def at_home(bias, queries, keys, values, token):
    return call(
        home_kernel,
        "at_home",
        [VMEM] * (3 * RING + 1) + [ANY],
        [((SLAB, D), f32, VMEM), ((SLAB, RING * HEAD), f32, VMEM)],
    )(bias, *queries, *keys, *values, token)


def last_keys_kernel(
    place_ref, normed_ref, gains_ref, w_ref, token_ref, o0, o1, o2, o3, cache_ref, held_ref, sems
):
    writes = []
    for part in (1, 2):
        project(normed_ref[...], w_ref, gains_ref, part, held_ref, (part - 1) * D)
        columns = pl.ds((part - 1) * D, D)
        writes.append(
            pltpu.make_async_copy(
                held_ref.at[:, columns], cache_ref.at[:, columns], sems.at[part - 1]
            )
        )
        writes[-1].start()
    dealt(place_ref, held_ref, 2, (o0, o1, o2, o3))
    for write in writes:
        write.wait()


def last_keys(where, normed, gains, w_qkv, token):
    return call(
        last_keys_kernel,
        "last_keys",
        [SMEM] + [VMEM] * 3 + [ANY],
        [((SLAB, 2 * WIDE), bf16, VMEM)] * RING + [((SLAB, 2 * D), bf16, HBM)],
        [pltpu.VMEM((SLAB, 2 * D), bf16), pltpu.SemaphoreType.DMA((2,))],
    )(where, normed, gains, w_qkv, token)


def hold_kernel(*refs):
    pass


def held(array, tokens):
    return call(
        hold_kernel,
        "hold",
        [ANY] * (1 + len(tokens)),
        [(array.shape, array.dtype, ANY)],
        aliases={0: 0},
    )(array, *tokens)[0]


def stack_kernel(*refs):
    blocks, out_ref = refs[:RING], refs[-1]
    first = blocks[0].shape[1] - 2 * WIDE
    for k, block in zip(ORDER, blocks):
        out_ref[k * SLAB : (k + 1) * SLAB, :] = block[:, first:]


def stack(blocks, token, us=0.1):
    return call(
        stack_kernel,
        "stack",
        [VMEM] * RING + [ANY],
        [((RING * SLAB, 2 * WIDE), bf16, VMEM)],
        us=us,
    )(*[blocks[k] for k in ORDER], token)[0]


def attend_kernel(token_ref, *refs, slots):
    n = len(slots)
    queries, olds, bias_ref, outs = refs[:n], refs[n : n + 4], refs[n + 4], refs[n + 5 :]
    lanes = lax.broadcasted_iota(jnp.int32, (SLAB, HEAD), 1)
    ones = jnp.ones((RING * SLAB, HEAD), bf16)
    lse = [jnp.zeros((SLAB, HEAD), f32)] * n
    for h in range(GROUP):
        here = slice(h * HEAD, (h + 1) * HEAD)
        there = slice(WIDE + h * HEAD, WIDE + (h + 1) * HEAD)
        keys = [old[:, here] for old in olds]
        values = [jnp.concatenate([old[:, there], ones], 1) for old in olds]
        joined = [query[:, here] for query in queries]
        joined = jnp.concatenate(joined, 0) if n > 1 else joined[0]
        products = [dots(joined, keys[a]) for a in range(4)]
        for i, slot in enumerate(slots):
            scores = []
            for a in range(4):
                row = a if a else 4 + slot
                scores.append(products[a][i * SLAB : (i + 1) * SLAB] + bias_ref[row : row + 1, :])
            highest = functools.reduce(
                jnp.maximum, [jnp.max(block, -1, keepdims=True) for block in scores]
            )
            both = 0.0
            for a in range(4):
                probs = jnp.exp2(scores[a] - highest).astype(bf16)
                both += jnp.dot(probs, values[a], preferred_element_type=f32)
            total = both[:, HEAD:]
            outs[i][:SLAB, here] = (both[:, :HEAD] / total).astype(bf16)
            lse[i] = jnp.where(lanes == h, highest + jnp.log2(total), lse[i])
    for i in range(n):
        rest = lse[i]
        packed = 0.0
        for part in range(3):
            piece = rest.astype(bf16).astype(f32)
            rest = rest - piece
            packed += pltpu.roll(piece, part * GROUP, 1) if part else piece
        outs[i][SLAB:, :HEAD] = packed.T[:EXTRA].astype(bf16)
        outs[i][SLAB:, HEAD:] = jnp.zeros((EXTRA, WIDE - HEAD), bf16)


def attend(queries, olds, bias, slots, token):
    return call(
        functools.partial(attend_kernel, slots=slots),
        "attend",
        [ANY] + [VMEM] * (len(slots) + 5),
        [((SLAB + EXTRA, WIDE), bf16, VMEM)] * len(slots),
        us=4,
    )(token, *[queries[k] for k in slots], *olds, bias)


def merged(away, summed_ref, lse_ref, k):
    rows = away[SLAB:, :HEAD].astype(f32)
    pieces = jnp.concatenate([rows, jnp.zeros((HEAD - EXTRA, HEAD), f32)], 0).T
    lse = (
        pieces + pltpu.roll(pieces, HEAD - GROUP, 1) + pltpu.roll(pieces, HEAD - 2 * GROUP, 1)
    )
    share = 1.0 / (1.0 + jnp.exp2(lse_ref[:, k * HEAD : (k + 1) * HEAD] - lse))
    heads = []
    for h in range(GROUP):
        here = slice(k * WIDE + h * HEAD, k * WIDE + (h + 1) * HEAD)
        part = share[:, h : h + 1]
        heads.append(
            part * away[:SLAB, h * HEAD : (h + 1) * HEAD].astype(f32)
            + (1.0 - part) * summed_ref[:, here]
        )
    return jnp.concatenate(heads, 1).astype(bf16)


def early_output_kernel(place_ref, a2, a1, a0, w_ref, summed_ref, lse_ref, out_ref):
    total = 0.0
    for k, away in enumerate((a0, a1, a2)):
        weight = w_ref[pl.ds(group_start(place_ref, k), WIDE), :]
        total += jnp.dot(
            merged(away, summed_ref, lse_ref, k), weight, preferred_element_type=f32
        )
    out_ref[...] = total


def early_output(where, away, summed, lse, w_out):
    return call(
        early_output_kernel,
        "early_output",
        [SMEM] + [VMEM] * 6,
        [((SLAB, D), f32, VMEM)],
        us=3,
    )(where, away[2], away[1], away[0], w_out, summed, lse)[0]


def output_kernel(
    place_ref, away, w_ref, summed_ref, lse_ref, early_ref, mixed_ref, gates_ref, out_ref, *edges, row
):
    weight = w_ref[pl.ds(group_start(place_ref, 3), WIDE), :]
    total = early_ref[...] + jnp.dot(
        merged(away, summed_ref, lse_ref, 3), weight, preferred_element_type=f32
    )
    gate = gates_ref[row : row + 1, :]
    out_ref[...] = (mixed_ref[...] + gate * total).astype(bf16)
    if edges:
        for edge_ref, start in zip(edges, edge_starts(place_ref[1])):
            edge_ref[...] = out_ref[pl.ds(start, FRAME), :]


def output(where, away, summed, lse, w_out, early, mixed, gates, row):
    edge = ((FRAME, D), bf16, VMEM)
    return call(
        functools.partial(output_kernel, row=row),
        "output",
        [SMEM] + [VMEM] * 7,
        [((SLAB, D), bf16, VMEM)] + ([edge, edge] if row + 1 < STEPS else []),
    )(where, away[3], w_out, summed, lse, early, mixed, gates)


def sent(block, k):
    return lax.ppermute(block, "patch", ring(k % RING)) if k % RING else block


def shards(latent, stale_kv, timesteps, counts, conv_weight, w_mod, w_qkv, q_gain, k_gain, w_out):
    own_slab = lax.axis_index("patch")
    y, z, c = own_slab // 8, (own_slab // 2) % RING, own_slab % 2
    where = jnp.stack([z, c, timesteps[0], timesteps[1], y]).astype(jnp.int32)
    to_core, to_chip, *pieces = prepare(where, latent, stale_kv)
    chip_rows = lax.ppermute(to_chip, "patch", NEXT_CHIP)
    core_rows = lax.ppermute(to_core, "patch", CORE)
    arrived = {k: sent(pieces[k], k) for k in ORDER}
    old = stack(arrived, arrived[0], us=8)
    old_y = lax.ppermute(old, "patch", ACROSS)
    old_core = lax.ppermute(old, "patch", CORE)
    mod, gains, mixed, *blocks = opening(
        where, latent, core_rows, chip_rows, conv_weight, q_gain, k_gain, w_mod, w_qkv, old
    )
    fresh = {k: sent(blocks[k], k) for k in ORDER}
    gates, bias = aside(where, counts, w_mod, mixed)
    summed, lse = at_home(bias, blocks, blocks, blocks, mixed)
    new = stack(fresh, lse)
    new_y = lax.ppermute(new, "patch", ACROSS)
    new_core = lax.ppermute(new, "patch", CORE)
    old_y = held(old_y, [new])
    olds = [old, old_core, old_y, lax.ppermute(old_y, "patch", CORE)]
    far = attend(fresh, olds, bias, (2, 1), new)
    (near,) = attend(fresh, olds, bias, (3,), far[0])
    (here,) = attend(fresh, olds, bias, (0,), near)
    away = {2: sent(far[0], -2), 1: sent(far[1], -1), 3: sent(near, -3), 0: here}
    early = early_output(where, away, summed, lse, w_out)
    state, to_core, to_chip = output(where, away, summed, lse, w_out, early, mixed, gates, 0)

    chip_rows = lax.ppermute(to_chip, "patch", NEXT_CHIP)
    core_rows = lax.ppermute(to_core, "patch", CORE)
    mixed, normed, *own = next_queries(
        where, state, core_rows, chip_rows, conv_weight, mod, gains, w_qkv, 1
    )
    queries = {k: sent(own[k], k) for k in ORDER}
    new_y = held(new_y, own[:1])
    olds = [new, new_core, new_y, lax.ppermute(new_y, "patch", CORE)]
    *pairs, cache = last_keys(where, normed, gains, w_qkv, normed)
    far = attend(queries, olds, bias, (2, 1), pairs[1])
    (near,) = attend(queries, olds, bias, (3,), far[0])
    (here,) = attend(queries, olds, bias, (0,), near)
    away = {2: sent(far[0], -2), 1: sent(far[1], -1), 3: sent(near, -3), 0: here}
    summed, lse = at_home(bias, own, pairs, pairs, normed)
    early = early_output(where, away, summed, lse, w_out)
    (state,) = output(where, away, summed, lse, w_out, early, mixed, gates, 1)
    return (state, cache)


def solution(mesh):
    rows = P(("req", "patch"), None)
    return jax.shard_map(
        shards,
        mesh=mesh,
        in_specs=(rows, rows, P("req"), P("req"), P(), P(), P(), P(), P(), P()),
        out_specs=(rows, rows),
        check_vma=False,
    )
```
